32 devices in a mesh: outer: 8 (over y, x, core), inner: 4 (over z).
Axes of the slice: x: 2, y: 2, z: 4, core: 2. Of those that a mesh axis runs over, the one named last changes fastest.
Arguments:
- queries: bfloat16 [4096, 1024], P(('outer', 'inner')), may hold values from -4.5 to 4.5
- key_vectors: bfloat16 [4096, 128], P(('outer', 'inner')), may hold values from -4.5 to 4.5
- value_vectors: bfloat16 [4096, 128], P(('outer', 'inner')), may hold values from -4 to 4
- grad_output: bfloat16 [4096, 1024], P(('outer', 'inner')), may hold values from -4 to 4
- positions: int32 [4096], P(('outer', 'inner')), may hold values from 0 to 4095, as said below
Outputs:
- attended: bfloat16 [4096, 1024], P(('outer', 'inner'))
- grad_queries: bfloat16 [4096, 1024], P(('outer', 'inner'))
- grad_keys: bfloat16 [4096, 128], P(('outer', 'inner'))
- grad_values: bfloat16 [4096, 128], P(('outer', 'inner'))
The draws below stay inside these ranges and needn't reach their ends.
Inputs may be any that keep to these rules, and one draw needn't show every extreme that they name: Each run of 512 rows holds the positions of one segment, 512 times the segment's number plus 0 to 511, each once. The 128 rows of one device hold two blocks of 64 ascending consecutive positions: block b of its segment first, then block 7 - b, where b runs over a permutation of 0 to 3 drawn anew for each segment.
All inputs are finite; a program needn't handle non-finite values.
Results may differ from the reference program's by a relative error of at most 0.03.
Values may be sent and summed in bfloat16 or wider, within the bound.
A program may use at most 64 MiB of HBM per device.

```python
import jax
import jax.numpy as jnp
from jax import lax

HEADS = 8
HEAD_DIM = 128
TOK_DEV = 128
GROUP = 4
SEGMENTS = 8
SPAN = 512
LENGTH = 4096


def draw_key_vectors(key, part):
    key = jax.random.fold_in(key, 7)
    rough = jnp.clip(jax.random.normal(key, (LENGTH, HEAD_DIM), jnp.float32), -4.5, 4.5)
    return rough.astype(jnp.bfloat16)


def draw_queries(key, part):
    key = jax.random.fold_in(key, 9)
    rough = jnp.clip(jax.random.normal(key, (LENGTH, HEADS * HEAD_DIM), jnp.float32), -4.5, 4.5)
    return rough.astype(jnp.bfloat16)


def draw_positions(key, part):
    key = jax.random.fold_in(key, 11)
    block_len = TOK_DEV // 2
    seg_keys = jax.random.split(key, SEGMENTS)
    order = jax.vmap(lambda seg_key: jax.random.permutation(seg_key, GROUP))(seg_keys)
    local = jnp.arange(TOK_DEV)
    in_first = local < block_len
    offsets = local % block_len
    block_ids = jnp.where(in_first[None, None, :], order[:, :, None], 2 * GROUP - 1 - order[:, :, None])
    result = jnp.arange(SEGMENTS)[:, None, None] * SPAN + block_ids * block_len + offsets[None, None, :]
    return result.reshape(LENGTH).astype(jnp.int32)


def block_scale(key, extent, pieces, smallest, top_value):
    def one(axis_at, parts):
        heights = jax.random.uniform(jax.random.fold_in(jax.random.fold_in(key, 6), axis_at), (parts,), jnp.float32, smallest / len(pieces), top_value / len(pieces))
        return jnp.repeat(jnp.exp(heights), extent[axis_at] // parts).reshape((-1,) + (1,) * (len(extent) - axis_at - 1))

    gain = one(*pieces[0])
    for cut in pieces[1:]:
        gain = gain * one(*cut)
    return gain


def gaussian(stream_key, extent, deviation, bound, pieces=(), kind=jnp.bfloat16):
    entries = deviation * jax.random.normal(stream_key, extent, jnp.float32)
    if pieces:
        entries = entries * block_scale(stream_key, extent, pieces, -0.22, 0.18)
    return jnp.clip(entries, -bound, bound).astype(kind)


def setup_inputs(seed: int = 0) -> dict:
    arg_keys = jax.random.split(jax.random.key(seed), 6)
    queries = draw_queries(jax.random.fold_in(arg_keys[5], 71), 0)
    key_vectors = draw_key_vectors(jax.random.fold_in(arg_keys[5], 71), 0)
    value_vectors = gaussian(arg_keys[2], (LENGTH, HEAD_DIM), 1.0, 4.0, ((0, 32),))
    grad_output = gaussian(arg_keys[3], (LENGTH, HEADS * HEAD_DIM), 1.0, 4.0, ((0, 32),))
    positions = draw_positions(jax.random.fold_in(arg_keys[5], 71), 0)
    return {"queries": queries, "key_vectors": key_vectors, "value_vectors": value_vectors, "grad_output": grad_output, "positions": positions}


masked_score = -1.0e30


def head_terms(query_head, grad_head, both_keys, both_values, allowed, score_scale):
    scores = jnp.dot(query_head, both_keys.T, preferred_element_type=jnp.float32) * score_scale
    scores = jnp.where(allowed, scores, masked_score)
    row_max = jnp.max(scores, axis=-1, keepdims=True)
    exp_scores = jnp.exp(scores - row_max)
    probs = exp_scores / jnp.sum(exp_scores, axis=-1, keepdims=True)
    weights = probs.astype(jnp.bfloat16)
    attn_out = jnp.dot(weights, both_values, preferred_element_type=jnp.float32).astype(jnp.bfloat16)
    row_delta = jnp.sum(grad_head.astype(jnp.float32) * attn_out.astype(jnp.float32), axis=-1, keepdims=True)
    prob_grad = jnp.dot(grad_head, both_values.T, preferred_element_type=jnp.float32)
    score_grad = (probs * (prob_grad - row_delta)).astype(jnp.bfloat16)
    query_grad = (jnp.dot(score_grad, both_keys, preferred_element_type=jnp.float32) * score_scale).astype(jnp.bfloat16)
    key_grad = jnp.dot(score_grad.T, query_head, preferred_element_type=jnp.float32) * score_scale
    value_grad = jnp.dot(weights.T, grad_head, preferred_element_type=jnp.float32)
    return attn_out, query_grad, key_grad, value_grad


def reference(queries, key_vectors, value_vectors, grad_output, positions):
    score_scale = float(HEAD_DIM) ** -0.5
    query_seg = queries.reshape(SEGMENTS, SPAN, HEADS, HEAD_DIM).transpose(0, 2, 1, 3)
    grad_seg = grad_output.reshape(SEGMENTS, SPAN, HEADS, HEAD_DIM).transpose(0, 2, 1, 3)
    key_seg = key_vectors.reshape(SEGMENTS, SPAN, HEAD_DIM)
    value_seg = value_vectors.reshape(SEGMENTS, SPAN, HEAD_DIM)
    zero_block = jnp.zeros((1, SPAN, HEAD_DIM), key_vectors.dtype)
    prev_keys = jnp.concatenate([zero_block, key_seg[:-1]], axis=0)
    prev_values = jnp.concatenate([zero_block, value_seg[:-1]], axis=0)
    pos_seg = positions.reshape(SEGMENTS, SPAN)
    has_prev = jnp.arange(SEGMENTS) > 0

    def segment_terms(items):
        query_heads, grad_heads, own_keys, own_values, prev_key, prev_value, seg_pos, prev_flag = items
        both_keys = jnp.concatenate([prev_key, own_keys], axis=0)
        both_values = jnp.concatenate([prev_value, own_values], axis=0)
        allowed = jnp.concatenate([jnp.broadcast_to(prev_flag, (SPAN, SPAN)),
                                   seg_pos[None, :] <= seg_pos[:, None]], axis=1)

        def per_head(head_items):
            return head_terms(head_items[0], head_items[1], both_keys, both_values, allowed, score_scale)

        attn_out, query_grad, key_grad, value_grad = lax.map(per_head, (query_heads, grad_heads))
        return attn_out, query_grad, jnp.sum(key_grad, axis=0), jnp.sum(value_grad, axis=0)

    attn_out, query_grad, key_total, value_total = lax.map(
        segment_terms, (query_seg, grad_seg, key_seg, value_seg, prev_keys, prev_values, pos_seg, has_prev))
    zero_terms = jnp.zeros((1, SPAN, HEAD_DIM), jnp.float32)
    key_back = jnp.concatenate([key_total[1:, :SPAN], zero_terms], axis=0)
    value_back = jnp.concatenate([value_total[1:, :SPAN], zero_terms], axis=0)
    grad_keys = (key_total[:, SPAN:] + key_back).reshape(LENGTH, HEAD_DIM).astype(jnp.bfloat16)
    grad_values = (value_total[:, SPAN:] + value_back).reshape(LENGTH, HEAD_DIM).astype(jnp.bfloat16)
    attended = attn_out.transpose(0, 2, 1, 3).reshape(LENGTH, HEADS * HEAD_DIM)
    grad_queries = query_grad.transpose(0, 2, 1, 3).reshape(LENGTH, HEADS * HEAD_DIM)
    return attended, grad_queries, grad_keys, grad_values
```

```python
import functools
import math

import jax
import jax.numpy as jnp
from jax import lax
from jax.experimental import pallas as pl
from jax.experimental.pallas import tpu as pltpu
from jax.sharding import PartitionSpec as P

masked_score = -1e30
MESH = pl.DeviceIdType.MESH
F32 = jnp.float32
BF16 = jnp.bfloat16


def dot_nt(a, b):
    return lax.dot_general(a, b, (((1,), (1,)), ((), ())), preferred_element_type=F32)


def dot_nn(a, b):
    return lax.dot_general(a, b, (((1,), (0,)), ((), ())), preferred_element_type=F32)


def kernel(
    segments, group, heads, dim, tok,
    q_ref, k_ref, v_ref, do_ref, pos_ref,
    att_ref, gq_ref, gk_ref, gv_ref,
    kv_own, kv_prev, qs, dos, q_t, do_t, s_ref, dp_ref, w_ref, g_send, g_recv, g_mine,
    kv_ssem, kv_rsem, g_ssem, g_rsem,
):
    seg = lax.axis_index("outer")
    me = lax.axis_index("inner")
    nxt = lax.rem(seg + 1, segments)
    prv = lax.rem(seg + segments - 1, segments)
    scale = float(dim) ** -0.5
    blocks = 2 * group

    barrier = pltpu.get_barrier_semaphore()
    partners = [(seg, lax.rem(me + d, group)) for d in range(1, group)]
    partners += [(nxt, lax.rem(me + d, group)) for d in range(group)]
    partners += [(prv, lax.rem(me + d, group)) for d in range(group)]
    for partner in partners:
        pl.semaphore_signal(barrier, inc=1, device_id=partner, device_id_type=MESH)

    pos = pos_ref[...]
    pos_hi = jnp.broadcast_to((pos >> 7).astype(F32), (8, tok))
    pos_lo = jnp.broadcast_to((pos & 127).astype(F32), (8, tok))
    kv_own[0, 0:tok, :] = k_ref[...]
    kv_own[0, tok : 2 * tok, :] = v_ref[...]
    kv_own[0, 2 * tok :, :] = jnp.concatenate([pos_hi, pos_lo], axis=0).astype(BF16)
    pl.semaphore_wait(barrier, len(partners))

    def kv_copy(block):
        d = block % group
        target = lax.rem(me + group - d, group)
        if block < group:
            src, dst, to = kv_own.at[0], kv_own.at[d], (seg, target)
        else:
            src, dst, to = kv_own.at[0, pl.ds(0, 2 * tok)], kv_prev.at[d], (nxt, target)
        return pltpu.make_async_remote_copy(
            src_ref=src, dst_ref=dst, send_sem=kv_ssem.at[block], recv_sem=kv_rsem.at[block],
            device_id=to, device_id_type=MESH,
        )

    kv_copies = {b: kv_copy(b) for b in range(1, blocks)}
    order = [group]
    for d in range(1, group):
        order += [d, group + d]
    for b in order:
        kv_copies[b].start()

    for h in range(heads):
        rows, cols = slice(h * tok, (h + 1) * tok), slice(h * dim, (h + 1) * dim)
        q_h, do_h = q_ref[:, cols], do_ref[:, cols]
        qs[rows, :] = q_h
        dos[rows, :] = do_h
        q_t[:, rows] = q_h.astype(F32).T.astype(BF16)
        do_t[:, rows] = do_h.astype(F32).T.astype(BF16)

    pos_col = jnp.broadcast_to(pos.astype(F32), (tok, tok)).T
    prev_bias = jnp.where(seg > 0, 0.0, masked_score).astype(F32)

    def keys_of(block):
        if block < group:
            return kv_own[block, 0:tok, :]
        return kv_prev[block - group, 0:tok, :]

    def values_of(block):
        if block < group:
            return kv_own[block, tok : 2 * tok, :]
        return kv_prev[block - group, tok : 2 * tok, :]

    def bias_of(block):
        if block >= group:
            return jnp.broadcast_to(prev_bias, (tok, tok))
        coded = kv_own[block, 2 * tok :, :].astype(F32)
        key_pos = coded[0:1, :] * 128.0 + coded[8:9, :]
        return jnp.where(key_pos <= pos_col, 0.0, masked_score)

    def cat(parts, axis):
        return parts[0] if len(parts) == 1 else jnp.concatenate(parts, axis=axis)

    steps = [[0], [1]] + [[b, b + 1] for b in range(2, blocks, 2)]
    for step in steps:
        for b in step:
            if b > 0:
                kv_copies[b].wait_recv()
        cols = slice(step[0] * tok, (step[-1] + 1) * tok)
        width = len(step) * tok
        score = dot_nt(qs[...], cat([keys_of(b) for b in step], 0))
        bias = cat([bias_of(b) for b in step], 1)
        score = score.reshape(heads, tok, width) + bias[None]
        s_ref[:, cols] = score.reshape(heads * tok, width)
        dp_ref[:, cols] = dot_nt(dos[...], cat([values_of(b) for b in step], 0))

    rate = scale * math.log2(math.e)
    for h in range(heads):
        rows = slice(h * tok, (h + 1) * tok)
        s = s_ref[rows, :]
        top = jnp.max(s, axis=1, keepdims=True)
        e = jnp.exp2((s - top) * rate)
        inv = 1.0 / jnp.sum(e, axis=1, keepdims=True)
        w_ref[rows, :] = (e * inv).astype(BF16)

    def grad_copy(block, part):
        d = block % group
        to = (seg if block < group else prv, lax.rem(me + d, group))
        return pltpu.make_async_remote_copy(
            src_ref=g_send.at[block, part], dst_ref=g_recv.at[block, part],
            send_sem=g_ssem.at[block, part], recv_sem=g_rsem.at[block, part],
            device_id=to, device_id_type=MESH,
        )

    grad_copies = {(b, p): grad_copy(b, p) for b in range(1, blocks) for p in range(2)}

    def send_grad(part, first, total):
        for n in range(2):
            b = first + n
            block = total[:, n * tok : (n + 1) * tok]
            if b == 0:
                g_mine[part] = block
            else:
                g_send[b, part] = block.astype(BF16)
                grad_copies[b, part].start()

    pairs = list(range(group, blocks, 2)) + list(range(group - 2, -1, -2))
    for first in pairs:
        cols = slice(first * tok, (first + 2) * tok)
        send_grad(1, first, dot_nn(do_t[...], w_ref[:, cols]))

    all_values = cat([values_of(b) for b in range(blocks)], 0)
    attended = dot_nn(w_ref[...], all_values).astype(BF16)
    delta = jnp.sum(dos[...].astype(F32) * attended.astype(F32), axis=1, keepdims=True)

    for first in pairs:
        cols = slice(first * tok, (first + 2) * tok)
        ds = (w_ref[:, cols].astype(F32) * (dp_ref[:, cols] - delta)).astype(BF16)
        w_ref[:, cols] = ds
        send_grad(0, first, dot_nn(q_t[...], ds) * scale)

    for h in range(heads):
        att_ref[:, h * dim : (h + 1) * dim] = attended[h * tok : (h + 1) * tok]

    all_keys = cat([keys_of(b) for b in range(blocks)], 0)
    gq = (dot_nn(w_ref[...], all_keys) * scale).astype(BF16)
    for h in range(heads):
        gq_ref[:, h * dim : (h + 1) * dim] = gq[h * tok : (h + 1) * tok]

    for part, out in ((1, gv_ref), (0, gk_ref)):
        total = g_mine[part]
        for b in range(1, blocks):
            grad_copies[b, part].wait_recv()
            total = total + g_recv[b, part].astype(F32)
        out[...] = total.T.astype(BF16)

    for b in range(1, blocks):
        kv_copies[b].wait_send()
        for part in range(2):
            grad_copies[b, part].wait_send()


def solution(mesh):
    segments, group = mesh.shape["outer"], mesh.shape["inner"]

    def body(queries, key_vectors, value_vectors, grad_output, positions):
        tok, full = queries.shape
        dim = key_vectors.shape[1]
        heads = full // dim
        blocks, rows = 2 * group, heads * tok
        keys = blocks * tok
        scratch = [
            ((group, 2 * tok + 16, dim), BF16),
            ((group, 2 * tok, dim), BF16),
            ((rows, dim), BF16),
            ((rows, dim), BF16),
            ((dim, rows), BF16),
            ((dim, rows), BF16),
            ((rows, keys), F32),
            ((rows, keys), F32),
            ((rows, keys), BF16),
            ((blocks, 2, dim, tok), BF16),
            ((blocks, 2, dim, tok), BF16),
            ((2, dim, tok), F32),
        ]
        used = sum(math.prod(s) * jnp.dtype(t).itemsize for s, t in scratch)
        vmem = pl.BlockSpec(memory_space=pltpu.VMEM)
        return pl.pallas_call(
            functools.partial(kernel, segments, group, heads, dim, tok),
            out_shape=[
                jax.ShapeDtypeStruct(queries.shape, BF16),
                jax.ShapeDtypeStruct(queries.shape, BF16),
                jax.ShapeDtypeStruct(key_vectors.shape, BF16),
                jax.ShapeDtypeStruct(key_vectors.shape, BF16),
            ],
            in_specs=[vmem] * 5,
            out_specs=[vmem] * 4,
            scratch_shapes=[pltpu.VMEM(s, t) for s, t in scratch]
            + [
                pltpu.SemaphoreType.DMA((blocks,)),
                pltpu.SemaphoreType.DMA((blocks,)),
                pltpu.SemaphoreType.DMA((blocks, 2)),
                pltpu.SemaphoreType.DMA((blocks, 2)),
            ],
            compiler_params=pltpu.CompilerParams(
                collective_id=0, has_side_effects=True, vmem_limit_bytes=used + (12 << 20)
            ),
            name="window_attention",
        )(queries, key_vectors, value_vectors, grad_output, positions.reshape(1, tok))

    rows = P(("outer", "inner"), None)
    return jax.shard_map(
        body,
        mesh=mesh,
        in_specs=(rows, rows, rows, rows, P(("outer", "inner"))),
        out_specs=(rows, rows, rows, rows),
        check_vma=False,
    )
```

```python
import functools
import math

import jax
import jax.numpy as jnp
from jax import lax
from jax.experimental import pallas as pl
from jax.experimental.pallas import tpu as pltpu
from jax.sharding import PartitionSpec as P

masked_score = -1e30
vmem_bytes = (64 << 20) - (600 << 10)
MESH = pl.DeviceIdType.MESH
F32 = jnp.float32
BF16 = jnp.bfloat16


def dot_nt(a, b):
    return lax.dot_general(a, b, (((1,), (1,)), ((), ())), preferred_element_type=F32)


def dot_nn(a, b):
    return lax.dot_general(a, b, (((1,), (0,)), ((), ())), preferred_element_type=F32)


def kernel(
    segments, group, heads, dim, tok,
    q_hbm, k_hbm, v_hbm, do_hbm, pos_hbm,
    att_hbm, gq_hbm, gk_hbm, gv_hbm,
    q_ref, do_ref, pos_ref, kv_own, kv_prev, qs, dos, q_t, do_t, s_ref, dp_ref, w_ref,
    p_send, p_recv, g_send, g_recv, g_mine, att_ref, gq_ref, gk_ref, gv_ref,
    in_sem, out_sem, kv_ssem, kv_rsem, fw_ssem, fw_rsem, p_ssem, p_rsem, g_ssem, g_rsem,
):
    seg = lax.axis_index("outer")
    me = lax.axis_index("inner")
    nxt = lax.rem(seg + 1, segments)
    prv = lax.rem(seg + segments - 1, segments)
    scale = float(dim) ** -0.5
    blocks = 2 * group

    loads = [
        pltpu.make_async_copy(k_hbm, kv_own.at[0, pl.ds(0, tok)], in_sem.at[0]),
        pltpu.make_async_copy(v_hbm, kv_own.at[0, pl.ds(tok, tok)], in_sem.at[1]),
        pltpu.make_async_copy(pos_hbm, pos_ref, in_sem.at[2]),
        pltpu.make_async_copy(q_hbm, q_ref, in_sem.at[3]),
        pltpu.make_async_copy(do_hbm, do_ref, in_sem.at[4]),
    ]
    stores = [
        pltpu.make_async_copy(att_ref, att_hbm, out_sem.at[0]),
        pltpu.make_async_copy(gq_ref, gq_hbm, out_sem.at[1]),
        pltpu.make_async_copy(gk_ref, gk_hbm, out_sem.at[2]),
        pltpu.make_async_copy(gv_ref, gv_hbm, out_sem.at[3]),
    ]
    for load in loads:
        load.start()

    barrier = pltpu.get_barrier_semaphore()
    partners = [(seg, lax.rem(me + d, group)) for d in range(1, group)] + [(nxt, me), (prv, me)]
    for partner in partners:
        pl.semaphore_signal(barrier, inc=1, device_id=partner, device_id_type=MESH)

    for load in loads[:3]:
        load.wait()
    pos = pos_ref[...]
    pos_hi = jnp.broadcast_to((pos >> 7).astype(F32), (8, tok))
    pos_lo = jnp.broadcast_to((pos & 127).astype(F32), (8, tok))
    kv_own[0, 2 * tok :, :] = jnp.concatenate([pos_hi, pos_lo], axis=0).astype(BF16)
    pl.semaphore_wait(barrier, len(partners))

    def kv_copy(d):
        return pltpu.make_async_remote_copy(
            src_ref=kv_own.at[0], dst_ref=kv_own.at[d],
            send_sem=kv_ssem.at[d], recv_sem=kv_rsem.at[d],
            device_id=(seg, lax.rem(me + group - d, group)), device_id_type=MESH,
        )

    def kv_forward(d):
        return pltpu.make_async_remote_copy(
            src_ref=kv_own.at[d, pl.ds(0, 2 * tok)], dst_ref=kv_prev.at[d],
            send_sem=fw_ssem.at[d], recv_sem=fw_rsem.at[d],
            device_id=(nxt, me), device_id_type=MESH,
        )

    kv_copies = {d: kv_copy(d) for d in range(1, group)}
    kv_forwards = [kv_forward(d) for d in range(group)]
    for d in range(1, group):
        kv_copies[d].start()
    kv_forwards[0].start()

    for load in loads[3:]:
        load.wait()
    for h in range(heads):
        rows, cols = slice(h * tok, (h + 1) * tok), slice(h * dim, (h + 1) * dim)
        q_h, do_h = q_ref[:, cols], do_ref[:, cols]
        qs[rows, :] = q_h
        dos[rows, :] = do_h
        q_t[:, rows] = q_h.astype(F32).T.astype(BF16)
        do_t[:, rows] = do_h.astype(F32).T.astype(BF16)

    pos_col = jnp.broadcast_to(pos.astype(F32), (tok, tok)).T
    prev_bias = jnp.where(seg > 0, 0.0, masked_score).astype(F32)

    def keys_of(block):
        if block < group:
            return kv_own[block, 0:tok, :]
        return kv_prev[block - group, 0:tok, :]

    def values_of(block):
        if block < group:
            return kv_own[block, tok : 2 * tok, :]
        return kv_prev[block - group, tok : 2 * tok, :]

    def bias_of(block):
        if block >= group:
            return jnp.broadcast_to(prev_bias, (tok, tok))
        coded = kv_own[block, 2 * tok :, :].astype(F32)
        key_pos = coded[0:1, :] * 128.0 + coded[8:9, :]
        return jnp.where(key_pos <= pos_col, 0.0, masked_score)

    def cat(parts, axis):
        return parts[0] if len(parts) == 1 else jnp.concatenate(parts, axis=axis)

    def score_step(step):
        cols = slice(step[0] * tok, (step[-1] + 1) * tok)
        width = len(step) * tok
        score = dot_nt(qs[...], cat([keys_of(b) for b in step], 0))
        bias = cat([bias_of(b) for b in step], 1)
        score = score.reshape(heads, tok, width) + bias[None]
        s_ref[:, cols] = score.reshape(heads * tok, width)
        dp_ref[:, cols] = dot_nt(dos[...], cat([values_of(b) for b in step], 0))

    score_step([0])
    for d in range(1, group):
        kv_copies[d].wait_recv()
        kv_forwards[d].start()
        if d == 1:
            score_step([1])
        elif d % 2 == 1:
            score_step([d - 1, d])
    for d in range(0, group, 2):
        kv_forwards[d].wait_recv()
        kv_forwards[d + 1].wait_recv()
        score_step([group + d, group + d + 1])

    rate = scale * math.log2(math.e)
    for h in range(heads):
        rows = slice(h * tok, (h + 1) * tok)
        s = s_ref[rows, :]
        top = jnp.max(s, axis=1, keepdims=True)
        e = jnp.exp2((s - top) * rate)
        inv = 1.0 / jnp.sum(e, axis=1, keepdims=True)
        w_ref[rows, :] = (e * inv).astype(BF16)

    def prev_copy(part, first):
        return pltpu.make_async_remote_copy(
            src_ref=p_send.at[part, pl.ds(first, 2)], dst_ref=p_recv.at[part, pl.ds(first, 2)],
            send_sem=p_ssem.at[part, first], recv_sem=p_rsem.at[part, first],
            device_id=(prv, me), device_id_type=MESH,
        )

    def grad_copy(part, d):
        return pltpu.make_async_remote_copy(
            src_ref=g_send.at[part, d], dst_ref=g_recv.at[part, d],
            send_sem=g_ssem.at[part, d], recv_sem=g_rsem.at[part, d],
            device_id=(seg, lax.rem(me + d, group)), device_id_type=MESH,
        )

    firsts = list(range(0, group, 2))
    prev_copies = {(p, f): prev_copy(p, f) for p in range(2) for f in firsts}
    grad_copies = {(p, d): grad_copy(p, d) for p in range(2) for d in range(1, group)}

    def columns(first):
        return slice(first * tok, (first + 2) * tok)

    def send_prev(part, first, total):
        for n in range(2):
            p_send[part, first + n] = total[:, n * tok : (n + 1) * tok].astype(BF16)
        prev_copies[part, first].start()

    def send_own(part, first, total):
        prev_copies[part, first].wait_recv()
        for n in (1, 0):
            d = first + n
            block = total[:, n * tok : (n + 1) * tok] + p_recv[part, d].astype(F32)
            if d == 0:
                g_mine[part] = block
            else:
                g_send[part, d] = block.astype(BF16)
                grad_copies[part, d].start()

    def key_terms(first):
        cols = columns(first)
        ds = (w_ref[:, cols].astype(F32) * (dp_ref[:, cols] - delta)).astype(BF16)
        w_ref[:, cols] = ds
        return dot_nn(q_t[...], ds) * scale

    for first in firsts:
        send_prev(1, first, dot_nn(do_t[...], w_ref[:, columns(group + first)]))

    all_values = cat([values_of(b) for b in range(blocks)], 0)
    attended = dot_nn(w_ref[...], all_values).astype(BF16)
    delta = jnp.sum(dos[...].astype(F32) * attended.astype(F32), axis=1, keepdims=True)
    for h in range(heads):
        att_ref[:, h * dim : (h + 1) * dim] = attended[h * tok : (h + 1) * tok]
    stores[0].start()

    for first in firsts[::-1]:
        send_own(1, first, dot_nn(do_t[...], w_ref[:, columns(first)]))
    for first in firsts:
        send_prev(0, first, key_terms(group + first))
    for first in firsts[::-1]:
        send_own(0, first, key_terms(first))

    all_keys = cat([keys_of(b) for b in range(blocks)], 0)
    gq = (dot_nn(w_ref[...], all_keys) * scale).astype(BF16)
    for h in range(heads):
        gq_ref[:, h * dim : (h + 1) * dim] = gq[h * tok : (h + 1) * tok]
    stores[1].start()

    for part, out, store in ((1, gv_ref, stores[3]), (0, gk_ref, stores[2])):
        total = g_mine[part]
        for d in range(1, group):
            grad_copies[part, d].wait_recv()
            total = total + g_recv[part, d].astype(F32)
        out[...] = total.T.astype(BF16)
        store.start()

    for copy in list(kv_copies.values()) + kv_forwards:
        copy.wait_send()
    for copy in list(prev_copies.values()) + list(grad_copies.values()):
        copy.wait_send()
    for store in stores:
        store.wait()


def store_kernel(*refs):
    count = (len(refs) - 1) // 2
    sems = refs[-1]
    copies = [
        pltpu.make_async_copy(refs[n], refs[count + n], sems.at[n]) for n in range(count)
    ]
    for copy in copies:
        copy.start()
    for copy in copies:
        copy.wait()


def solution(mesh):
    segments, group = mesh.shape["outer"], mesh.shape["inner"]

    def body(queries, key_vectors, value_vectors, grad_output, positions):
        tok, full = queries.shape
        dim = key_vectors.shape[1]
        heads = full // dim
        blocks, rows = 2 * group, heads * tok
        keys = blocks * tok
        scratch = [
            ((tok, full), BF16),
            ((tok, full), BF16),
            ((1, tok), jnp.int32),
            ((group, 2 * tok + 16, dim), BF16),
            ((group, 2 * tok, dim), BF16),
            ((rows, dim), BF16),
            ((rows, dim), BF16),
            ((dim, rows), BF16),
            ((dim, rows), BF16),
            ((rows, keys), F32),
            ((rows, keys), F32),
            ((rows, keys), BF16),
            ((2, group, dim, tok), BF16),
            ((2, group, dim, tok), BF16),
            ((2, group, dim, tok), BF16),
            ((2, group, dim, tok), BF16),
            ((2, dim, tok), F32),
            ((tok, full), BF16),
            ((tok, full), BF16),
            ((tok, dim), BF16),
            ((tok, dim), BF16),
        ]
        hbm = pl.BlockSpec(memory_space=pl.ANY)
        results = [
            jax.ShapeDtypeStruct(queries.shape, BF16),
            jax.ShapeDtypeStruct(queries.shape, BF16),
            jax.ShapeDtypeStruct(key_vectors.shape, BF16),
            jax.ShapeDtypeStruct(key_vectors.shape, BF16),
        ]
        sem = pltpu.SemaphoreType.DMA
        made = pl.pallas_call(
            functools.partial(kernel, segments, group, heads, dim, tok),
            out_shape=results,
            in_specs=[hbm] * 5,
            out_specs=[hbm] * 4,
            scratch_shapes=[pltpu.VMEM(s, t) for s, t in scratch]
            + [sem((5,)), sem((4,))]
            + [sem((group,))] * 4
            + [sem((2, group))] * 4,
            compiler_params=pltpu.CompilerParams(
                collective_id=0, has_side_effects=True, vmem_limit_bytes=vmem_bytes
            ),
            name="window_attention",
        )(queries, key_vectors, value_vectors, grad_output, positions.reshape(1, tok))
        return pl.pallas_call(
            store_kernel,
            out_shape=results,
            in_specs=[hbm] * 4,
            out_specs=[hbm] * 4,
            scratch_shapes=[sem((4,))],
            name="store_results",
        )(*made)

    rows = P(("outer", "inner"), None)
    return jax.shard_map(
        body,
        mesh=mesh,
        in_specs=(rows, rows, rows, rows, P(("outer", "inner"))),
        out_specs=(rows, rows, rows, rows),
        check_vma=False,
    )
```

```python
import functools
import math

import jax
import jax.numpy as jnp
from jax import lax
from jax.experimental import pallas as pl
from jax.experimental.pallas import tpu as pltpu
from jax.sharding import PartitionSpec as P

masked_score = -1e30
vmem_bytes = (64 << 20) - (600 << 10)
MESH = pl.DeviceIdType.MESH
F32 = jnp.float32
BF16 = jnp.bfloat16


def dot_nt(a, b):
    return lax.dot_general(a, b, (((1,), (1,)), ((), ())), preferred_element_type=F32)


def dot_nn(a, b):
    return lax.dot_general(a, b, (((1,), (0,)), ((), ())), preferred_element_type=F32)


def kernel(
    segments, group, heads, dim, tok,
    q_hbm, k_hbm, v_hbm, do_hbm, pos_hbm,
    att_hbm, gq_hbm, mine_hbm, recv_hbm,
    q_ref, do_ref, pos_ref, k_own, v_own, k_prev, v_prev, qs, dos, q_t, do_t, s_ref, dp_ref, w_ref,
    p_send, p_recv, g_send, g_mine, att_ref, gq_ref,
    in_sem, out_sem, k_ssem, k_rsem, v_ssem, v_rsem, kf_ssem, kf_rsem, vf_ssem, vf_rsem,
    p_ssem, p_rsem, g_ssem, g_rsem,
):
    seg = lax.axis_index("outer")
    me = lax.axis_index("inner")
    nxt = lax.rem(seg + 1, segments)
    prv = lax.rem(seg + segments - 1, segments)
    scale = float(dim) ** -0.5
    blocks = 2 * group

    loads = [
        pltpu.make_async_copy(k_hbm, k_own.at[0, pl.ds(0, tok)], in_sem.at[0]),
        pltpu.make_async_copy(pos_hbm, pos_ref, in_sem.at[1]),
        pltpu.make_async_copy(v_hbm, v_own.at[0], in_sem.at[2]),
        pltpu.make_async_copy(q_hbm, q_ref, in_sem.at[3]),
        pltpu.make_async_copy(do_hbm, do_ref, in_sem.at[4]),
    ]
    stores = [
        pltpu.make_async_copy(att_ref, att_hbm, out_sem.at[0]),
        pltpu.make_async_copy(gq_ref, gq_hbm, out_sem.at[1]),
        pltpu.make_async_copy(g_mine.at[0], mine_hbm.at[0], out_sem.at[2]),
        pltpu.make_async_copy(g_mine.at[1], mine_hbm.at[1], out_sem.at[3]),
    ]
    for load in loads:
        load.start()

    barrier = pltpu.get_barrier_semaphore()
    partners = [(seg, lax.rem(me + d, group)) for d in range(1, group)] + [(nxt, me), (prv, me)]
    for partner in partners:
        pl.semaphore_signal(barrier, inc=1, device_id=partner, device_id_type=MESH)

    for load in loads[:3]:
        load.wait()
    pos = pos_ref[...]
    pos_hi = jnp.broadcast_to((pos >> 7).astype(F32), (8, tok))
    pos_lo = jnp.broadcast_to((pos & 127).astype(F32), (8, tok))
    k_own[0, tok:, :] = jnp.concatenate([pos_hi, pos_lo], axis=0).astype(BF16)
    pl.semaphore_wait(barrier, len(partners))

    def gather(buf, ssem, rsem, d):
        return pltpu.make_async_remote_copy(
            src_ref=buf.at[0], dst_ref=buf.at[d], send_sem=ssem.at[d], recv_sem=rsem.at[d],
            device_id=(seg, lax.rem(me + group - d, group)), device_id_type=MESH,
        )

    def forward(src, dst, ssem, rsem, d):
        return pltpu.make_async_remote_copy(
            src_ref=src.at[d, pl.ds(0, tok)], dst_ref=dst.at[d],
            send_sem=ssem.at[d], recv_sem=rsem.at[d],
            device_id=(nxt, me), device_id_type=MESH,
        )

    others = range(1, group)
    k_copies = {d: gather(k_own, k_ssem, k_rsem, d) for d in others}
    v_copies = {d: gather(v_own, v_ssem, v_rsem, d) for d in others}
    k_forwards = [forward(k_own, k_prev, kf_ssem, kf_rsem, d) for d in range(group)]
    v_forwards = [forward(v_own, v_prev, vf_ssem, vf_rsem, d) for d in range(group)]
    for d in others:
        k_copies[d].start()
    k_forwards[0].start()

    for load in loads[3:]:
        load.wait()
    for h in range(heads):
        rows, cols = slice(h * tok, (h + 1) * tok), slice(h * dim, (h + 1) * dim)
        q_h, do_h = q_ref[:, cols], do_ref[:, cols]
        qs[rows, :] = q_h
        dos[rows, :] = do_h
        q_t[:, rows] = q_h.astype(F32).T.astype(BF16)
        do_t[:, rows] = do_h.astype(F32).T.astype(BF16)
    for d in others:
        v_copies[d].start()
    v_forwards[0].start()

    pos_col = jnp.broadcast_to(pos.astype(F32), (tok, tok)).T
    prev_bias = jnp.where(seg > 0, 0.0, masked_score).astype(F32)

    def keys_of(block):
        return k_own[block, 0:tok, :] if block < group else k_prev[block - group]

    def values_of(block):
        return v_own[block] if block < group else v_prev[block - group]

    def bias_of(block):
        if block >= group:
            return jnp.broadcast_to(prev_bias, (tok, tok))
        coded = k_own[block, tok:, :].astype(F32)
        key_pos = coded[0:1, :] * 128.0 + coded[8:9, :]
        return jnp.where(key_pos <= pos_col, 0.0, masked_score)

    def cat(parts, axis):
        return parts[0] if len(parts) == 1 else jnp.concatenate(parts, axis=axis)

    def columns(step):
        return slice(step[0] * tok, (step[-1] + 1) * tok)

    def score_step(step):
        width = len(step) * tok
        score = dot_nt(qs[...], cat([keys_of(b) for b in step], 0))
        bias = cat([bias_of(b) for b in step], 1)
        score = score.reshape(heads, tok, width) + bias[None]
        s_ref[:, columns(step)] = score.reshape(heads * tok, width)

    def grad_step(step):
        dp_ref[:, columns(step)] = dot_nt(dos[...], cat([values_of(b) for b in step], 0))

    score_step([0])
    for d in others:
        k_copies[d].wait_recv()
        k_forwards[d].start()
        if d == 1:
            score_step([1])
        elif d % 2 == 1:
            score_step([d - 1, d])

    rate = scale * math.log2(math.e)
    own, prev = slice(0, group * tok), slice(group * tok, blocks * tok)
    own_top, own_sum = [], []
    for h in range(heads):
        rows = slice(h * tok, (h + 1) * tok)
        s = s_ref[rows, own]
        top = jnp.max(s, axis=1, keepdims=True)
        e = jnp.exp2((s - top) * rate)
        s_ref[rows, own] = e
        own_top.append(top)
        own_sum.append(jnp.sum(e, axis=1, keepdims=True))

    for d in others:
        v_copies[d].wait_recv()
        v_forwards[d].start()
    for d in range(0, group, 2):
        grad_step([d, d + 1])

    for d in range(0, group, 2):
        k_forwards[d].wait_recv()
        k_forwards[d + 1].wait_recv()
        score_step([group + d, group + d + 1])
    for h in range(heads):
        rows = slice(h * tok, (h + 1) * tok)
        s = s_ref[rows, prev]
        top = jnp.maximum(own_top[h], jnp.max(s, axis=1, keepdims=True))
        e = jnp.exp2((s - top) * rate)
        shrink = jnp.exp2((own_top[h] - top) * rate)
        inv = 1.0 / (own_sum[h] * shrink + jnp.sum(e, axis=1, keepdims=True))
        w_ref[rows, prev] = (e * inv).astype(BF16)
        w_ref[rows, own] = (s_ref[rows, own] * (shrink * inv)).astype(BF16)

    def prev_copy(part, first):
        return pltpu.make_async_remote_copy(
            src_ref=p_send.at[part, pl.ds(first, 2)], dst_ref=p_recv.at[part, pl.ds(first, 2)],
            send_sem=p_ssem.at[part, first], recv_sem=p_rsem.at[part, first],
            device_id=(prv, me), device_id_type=MESH,
        )

    def grad_copy(part, d):
        return pltpu.make_async_remote_copy(
            src_ref=g_send.at[part, d], dst_ref=recv_hbm.at[part, d - 1],
            send_sem=g_ssem.at[part, d], recv_sem=g_rsem.at[part, d],
            device_id=(seg, lax.rem(me + d, group)), device_id_type=MESH,
        )

    firsts = list(range(0, group, 2))
    prev_copies = {(p, f): prev_copy(p, f) for p in range(2) for f in firsts}
    grad_copies = {(p, d): grad_copy(p, d) for p in range(2) for d in others}

    def pair(first):
        return columns([first, first + 1])

    def send_prev(part, first, total):
        for n in range(2):
            p_send[part, first + n] = total[:, n * tok : (n + 1) * tok].astype(BF16)
        prev_copies[part, first].start()

    def send_own(part, first, total):
        prev_copies[part, first].wait_recv()
        for n in (1, 0):
            d = first + n
            block = total[:, n * tok : (n + 1) * tok] + p_recv[part, d].astype(F32)
            if d == 0:
                g_mine[part] = block
                stores[2 + part].start()
            else:
                g_send[part, d] = block.astype(BF16)
                grad_copies[part, d].start()

    def key_terms(first):
        cols = pair(first)
        ds = (w_ref[:, cols].astype(F32) * (dp_ref[:, cols] - delta)).astype(BF16)
        w_ref[:, cols] = ds
        return dot_nn(q_t[...], ds) * scale

    for first in firsts:
        send_prev(1, first, dot_nn(do_t[...], w_ref[:, pair(group + first)]))

    for d in range(0, group, 2):
        v_forwards[d].wait_recv()
        v_forwards[d + 1].wait_recv()
        grad_step([group + d, group + d + 1])
    all_values = cat([values_of(b) for b in range(blocks)], 0)
    attended = dot_nn(w_ref[...], all_values).astype(BF16)
    delta = jnp.sum(dos[...].astype(F32) * attended.astype(F32), axis=1, keepdims=True)
    for h in range(heads):
        att_ref[:, h * dim : (h + 1) * dim] = attended[h * tok : (h + 1) * tok]
    stores[0].start()

    for first in firsts[::-1]:
        send_own(1, first, dot_nn(do_t[...], w_ref[:, pair(first)]))
    for first in firsts:
        send_prev(0, first, key_terms(group + first))
    for first in firsts[::-1]:
        send_own(0, first, key_terms(first))

    all_keys = cat([keys_of(b) for b in range(blocks)], 0)
    gq = (dot_nn(w_ref[...], all_keys) * scale).astype(BF16)
    for h in range(heads):
        gq_ref[:, h * dim : (h + 1) * dim] = gq[h * tok : (h + 1) * tok]
    stores[1].start()

    for copy in list(k_copies.values()) + list(v_copies.values()) + k_forwards + v_forwards:
        copy.wait_send()
    for copy in list(prev_copies.values()) + list(grad_copies.values()):
        copy.wait_send()
    for store in stores:
        store.wait()
    for copy in grad_copies.values():
        copy.wait_recv()


def store_kernel(
    group,
    att_hbm, gq_hbm, mine_hbm, recv_hbm, att_out, gq_out, gk_out, gv_out,
    att_ref, gq_ref, mine_ref, recv_ref, gk_ref, gv_ref, in_sem, out_sem,
):
    moves = ((mine_hbm, mine_ref), (recv_hbm, recv_ref), (att_hbm, att_ref), (gq_hbm, gq_ref))
    loads = [pltpu.make_async_copy(a, b, in_sem.at[n]) for n, (a, b) in enumerate(moves)]
    moves = ((att_ref, att_out), (gq_ref, gq_out), (gk_ref, gk_out), (gv_ref, gv_out))
    stores = [pltpu.make_async_copy(a, b, out_sem.at[n]) for n, (a, b) in enumerate(moves)]
    for load in loads:
        load.start()
    loads[0].wait()
    loads[1].wait()
    for part, out in ((0, gk_ref), (1, gv_ref)):
        total = mine_ref[part]
        for d in range(group - 1):
            total = total + recv_ref[part, d].astype(F32)
        out[...] = total.T.astype(BF16)
        stores[2 + part].start()
    for n in range(2):
        loads[2 + n].wait()
        stores[n].start()
    for store in stores:
        store.wait()


def solution(mesh):
    segments, group = mesh.shape["outer"], mesh.shape["inner"]

    def body(queries, key_vectors, value_vectors, grad_output, positions):
        tok, full = queries.shape
        dim = key_vectors.shape[1]
        heads = full // dim
        blocks, rows = 2 * group, heads * tok
        keys = blocks * tok
        wide, narrow = (tok, full), (tok, dim)
        scratch = [
            (wide, BF16),
            (wide, BF16),
            ((1, tok), jnp.int32),
            ((group, tok + 16, dim), BF16),
            ((group, tok, dim), BF16),
            ((group, tok, dim), BF16),
            ((group, tok, dim), BF16),
            ((rows, dim), BF16),
            ((rows, dim), BF16),
            ((dim, rows), BF16),
            ((dim, rows), BF16),
            ((rows, keys), F32),
            ((rows, keys), F32),
            ((rows, keys), BF16),
            ((2, group, dim, tok), BF16),
            ((2, group, dim, tok), BF16),
            ((2, group, dim, tok), BF16),
            ((2, dim, tok), F32),
            (wide, BF16),
            (wide, BF16),
        ]
        made = [(wide, BF16), (wide, BF16), ((2, dim, tok), F32), ((2, group - 1, dim, tok), BF16)]
        results = [(wide, BF16), (wide, BF16), (narrow, BF16), (narrow, BF16)]
        hbm = pl.BlockSpec(memory_space=pl.ANY)
        sem = pltpu.SemaphoreType.DMA
        partial = pl.pallas_call(
            functools.partial(kernel, segments, group, heads, dim, tok),
            out_shape=[jax.ShapeDtypeStruct(s, t) for s, t in made],
            in_specs=[hbm] * 5,
            out_specs=[hbm] * 4,
            scratch_shapes=[pltpu.VMEM(s, t) for s, t in scratch]
            + [sem((5,)), sem((4,))]
            + [sem((group,))] * 8
            + [sem((2, group))] * 4,
            compiler_params=pltpu.CompilerParams(
                collective_id=0, has_side_effects=True, vmem_limit_bytes=vmem_bytes
            ),
            name="window_attention",
        )(queries, key_vectors, value_vectors, grad_output, positions.reshape(1, tok))
        return pl.pallas_call(
            functools.partial(store_kernel, group),
            out_shape=[jax.ShapeDtypeStruct(s, t) for s, t in results],
            in_specs=[hbm] * 4,
            out_specs=[hbm] * 4,
            scratch_shapes=[pltpu.VMEM(s, t) for s, t in made + results[2:]] + [sem((4,))] * 2,
            compiler_params=pltpu.CompilerParams(vmem_limit_bytes=vmem_bytes),
            name="store_results",
        )(*partial)

    rows = P(("outer", "inner"), None)
    return jax.shard_map(
        body,
        mesh=mesh,
        in_specs=(rows, rows, rows, rows, P(("outer", "inner"))),
        out_specs=(rows, rows, rows, rows),
        check_vma=False,
    )
```

```python
import functools
import math

import jax
import jax.numpy as jnp
from jax import lax
from jax.experimental import pallas as pl
from jax.experimental.pallas import tpu as pltpu
from jax.sharding import PartitionSpec as P

masked_score = -1e30
vmem_bytes = (64 << 20) - (600 << 10)
MESH = pl.DeviceIdType.MESH
F32 = jnp.float32
BF16 = jnp.bfloat16


def dot_nt(a, b):
    return lax.dot_general(a, b, (((1,), (1,)), ((), ())), preferred_element_type=F32)


def dot_nn(a, b):
    return lax.dot_general(a, b, (((1,), (0,)), ((), ())), preferred_element_type=F32)


def kernel(
    segments, group, heads, dim, tok,
    q_hbm, k_hbm, v_hbm, do_hbm, pos_hbm,
    att_hbm, gq_hbm, mine_hbm, recv_hbm,
    q_ref, do_ref, pos_ref, k_own, v_own, k_prev, v_prev, qs, dos, q_t, do_t, s_ref, dp_ref, w_ref,
    p_send, p_recv, g_send, g_mine, att_ref, gq_ref, pos_col, top_ref, sum_ref, delta_ref,
    in_sem, out_sem, k_ssem, k_rsem, v_ssem, v_rsem, kf_ssem, kf_rsem, vf_ssem, vf_rsem,
    p_ssem, p_rsem, g_ssem, g_rsem,
):
    seg = lax.axis_index("outer")
    me = lax.axis_index("inner")
    nxt = lax.rem(seg + 1, segments)
    prv = lax.rem(seg + segments - 1, segments)
    scale = float(dim) ** -0.5
    blocks = 2 * group

    loads = [
        pltpu.make_async_copy(k_hbm, k_own.at[0, pl.ds(0, tok)], in_sem.at[0]),
        pltpu.make_async_copy(pos_hbm, pos_ref, in_sem.at[1]),
        pltpu.make_async_copy(v_hbm, v_own.at[0], in_sem.at[2]),
        pltpu.make_async_copy(q_hbm, q_ref, in_sem.at[3]),
        pltpu.make_async_copy(do_hbm, do_ref, in_sem.at[4]),
    ]
    stores = [
        pltpu.make_async_copy(att_ref, att_hbm, out_sem.at[0]),
        pltpu.make_async_copy(gq_ref, gq_hbm, out_sem.at[1]),
        pltpu.make_async_copy(g_mine.at[0], mine_hbm.at[0], out_sem.at[2]),
        pltpu.make_async_copy(g_mine.at[1], mine_hbm.at[1], out_sem.at[3]),
    ]
    for load in loads:
        load.start()

    barrier = pltpu.get_barrier_semaphore()
    partners = [(seg, lax.rem(me + d, group)) for d in range(1, group)] + [(nxt, me), (prv, me)]
    for partner in partners:
        pl.semaphore_signal(barrier, inc=1, device_id=partner, device_id_type=MESH)

    for load in loads[:3]:
        load.wait()
    pos = pos_ref[...]
    pos_hi = jnp.broadcast_to((pos >> 7).astype(F32), (8, tok))
    pos_lo = jnp.broadcast_to((pos & 127).astype(F32), (8, tok))
    k_own[0, tok:, :] = jnp.concatenate([pos_hi, pos_lo], axis=0).astype(BF16)
    pl.semaphore_wait(barrier, len(partners))

    def gather(buf, ssem, rsem, d):
        return pltpu.make_async_remote_copy(
            src_ref=buf.at[0], dst_ref=buf.at[d], send_sem=ssem.at[d], recv_sem=rsem.at[d],
            device_id=(seg, lax.rem(me + group - d, group)), device_id_type=MESH,
        )

    def forward(src, dst, ssem, rsem, d):
        return pltpu.make_async_remote_copy(
            src_ref=src.at[d, pl.ds(0, tok)], dst_ref=dst.at[d],
            send_sem=ssem.at[d], recv_sem=rsem.at[d],
            device_id=(nxt, me), device_id_type=MESH,
        )

    others = range(1, group)
    k_copies = {d: gather(k_own, k_ssem, k_rsem, d) for d in others}
    v_copies = {d: gather(v_own, v_ssem, v_rsem, d) for d in others}
    k_forwards = [forward(k_own, k_prev, kf_ssem, kf_rsem, d) for d in range(group)]
    v_forwards = [forward(v_own, v_prev, vf_ssem, vf_rsem, d) for d in range(group)]
    for d in others:
        k_copies[d].start()
    k_forwards[0].start()

    for load in loads[3:]:
        load.wait()

    @pl.loop(0, heads)
    def _(h):
        rows, cols = pl.ds(h * tok, tok), pl.ds(h * dim, dim)
        q_h, do_h = q_ref[:, cols], do_ref[:, cols]
        qs[rows, :] = q_h
        dos[rows, :] = do_h
        q_t[:, rows] = q_h.astype(F32).T.astype(BF16)
        do_t[:, rows] = do_h.astype(F32).T.astype(BF16)

    for d in others:
        v_copies[d].start()
    v_forwards[0].start()

    pos_col[...] = jnp.broadcast_to(pos.astype(F32), (tok, tok)).T
    prev_bias = jnp.where(seg > 0, 0.0, masked_score).astype(F32)
    own, prev = slice(0, group * tok), slice(group * tok, blocks * tok)
    pairs, span = group // 2, 2 * tok

    @pl.loop(0, group)
    def _(d):
        @pl.when(d > 0)
        def _():
            gather(k_own, k_ssem, k_rsem, d).wait_recv()
            forward(k_own, k_prev, kf_ssem, kf_rsem, d).start()

        coded = k_own[d, tok:, :].astype(F32)
        key_pos = coded[0:1, :] * 128.0 + coded[8:9, :]
        bias = jnp.where(key_pos <= pos_col[...], 0.0, masked_score)
        score = dot_nt(qs[...], k_own[d, 0:tok, :]).reshape(heads, tok, tok) + bias[None]
        s_ref[:, pl.ds(d * tok, tok)] = score.reshape(heads * tok, tok)

    rate = scale * math.log2(math.e)

    @pl.loop(0, heads)
    def _(h):
        rows = pl.ds(h * tok, tok)
        s = s_ref[rows, own]
        top = jnp.max(s, axis=1, keepdims=True)
        e = jnp.exp2((s - top) * rate)
        s_ref[rows, own] = e
        top_ref[rows, :] = top
        sum_ref[rows, :] = jnp.sum(e, axis=1, keepdims=True)

    for d in others:
        v_copies[d].wait_recv()
        v_forwards[d].start()

    @pl.loop(0, pairs)
    def _(p):
        values = v_own[pl.ds(2 * p, 2)].reshape(span, dim)
        dp_ref[:, pl.ds(p * span, span)] = dot_nt(dos[...], values)

    @pl.loop(0, pairs)
    def _(p):
        for n in range(2):
            forward(k_own, k_prev, kf_ssem, kf_rsem, 2 * p + n).wait_recv()
        score = dot_nt(qs[...], k_prev[pl.ds(2 * p, 2)].reshape(span, dim))
        s_ref[:, pl.ds((pairs + p) * span, span)] = score + prev_bias

    @pl.loop(0, heads)
    def _(h):
        rows = pl.ds(h * tok, tok)
        s = s_ref[rows, prev]
        own_top = top_ref[rows, :]
        top = jnp.maximum(own_top, jnp.max(s, axis=1, keepdims=True))
        e = jnp.exp2((s - top) * rate)
        shrink = jnp.exp2((own_top - top) * rate)
        inv = 1.0 / (sum_ref[rows, :] * shrink + jnp.sum(e, axis=1, keepdims=True))
        w_ref[rows, prev] = (e * inv).astype(BF16)
        w_ref[rows, own] = (s_ref[rows, own] * (shrink * inv)).astype(BF16)

    def prev_copy(part, p):
        two = pl.ds(2 * p, 2)
        return pltpu.make_async_remote_copy(
            src_ref=p_send.at[part, two], dst_ref=p_recv.at[part, two],
            send_sem=p_ssem.at[part, p], recv_sem=p_rsem.at[part, p],
            device_id=(prv, me), device_id_type=MESH,
        )

    def grad_copy(part, d):
        return pltpu.make_async_remote_copy(
            src_ref=g_send.at[part, d], dst_ref=recv_hbm.at[part, d - 1],
            send_sem=g_ssem.at[part, d], recv_sem=g_rsem.at[part, d],
            device_id=(seg, lax.rem(me + d, group)), device_id_type=MESH,
        )

    def terms(part, p):
        cols = pl.ds(p * span, span)
        if part == 1:
            return dot_nn(do_t[...], w_ref[:, cols])
        ds = (w_ref[:, cols].astype(F32) * (dp_ref[:, cols] - delta_ref[...])).astype(BF16)
        w_ref[:, cols] = ds
        return dot_nn(q_t[...], ds) * scale

    def prev_terms(part):
        @pl.loop(0, pairs)
        def _(p):
            total = terms(part, pairs + p)
            for n in range(2):
                p_send[part, 2 * p + n] = total[:, n * tok : (n + 1) * tok].astype(BF16)
            prev_copy(part, p).start()

    def own_terms(part):
        @pl.loop(0, pairs)
        def _(step):
            p = pairs - 1 - step
            total = terms(part, p)
            prev_copy(part, p).wait_recv()

            def send(n):
                d = 2 * p + n
                block = total[:, n * tok : (n + 1) * tok] + p_recv[part, d].astype(F32)
                g_send[part, d] = block.astype(BF16)
                grad_copy(part, d).start()

            send(1)

            @pl.when(p > 0)
            def _():
                send(0)

            @pl.when(p == 0)
            def _():
                g_mine[part] = total[:, 0:tok] + p_recv[part, 0].astype(F32)
                stores[2 + part].start()

    prev_terms(1)

    @pl.loop(0, pairs)
    def _(p):
        for n in range(2):
            forward(v_own, v_prev, vf_ssem, vf_rsem, 2 * p + n).wait_recv()
        values = v_prev[pl.ds(2 * p, 2)].reshape(span, dim)
        dp_ref[:, pl.ds((pairs + p) * span, span)] = dot_nt(dos[...], values)

    def weighted(rows, own_part, prev_part):
        own_part = own_part.reshape(group * tok, dim)
        prev_part = prev_part.reshape(group * tok, dim)
        return dot_nn(w_ref[rows, own], own_part) + dot_nn(w_ref[rows, prev], prev_part)

    @pl.loop(0, heads // 2)
    def _(c):
        rows = pl.ds(c * span, span)
        attended = weighted(rows, v_own[...], v_prev[...]).astype(BF16)
        product = dos[rows, :].astype(F32) * attended.astype(F32)
        delta_ref[rows, :] = jnp.sum(product, axis=1, keepdims=True)
        for n in range(2):
            att_ref[:, pl.ds((2 * c + n) * dim, dim)] = attended[n * tok : (n + 1) * tok]

    stores[0].start()
    own_terms(1)
    prev_terms(0)
    own_terms(0)

    @pl.loop(0, heads // 2)
    def _(c):
        rows = pl.ds(c * span, span)
        gq = (weighted(rows, k_own[:, 0:tok, :], k_prev[...]) * scale).astype(BF16)
        for n in range(2):
            gq_ref[:, pl.ds((2 * c + n) * dim, dim)] = gq[n * tok : (n + 1) * tok]

    stores[1].start()
    grads = [grad_copy(part, d) for part in range(2) for d in others]
    returns = [prev_copy(part, p) for part in range(2) for p in range(pairs)]
    sent = list(k_copies.values()) + list(v_copies.values()) + k_forwards + v_forwards
    for copy in sent + returns + grads:
        copy.wait_send()
    for store in stores:
        store.wait()
    for copy in grads:
        copy.wait_recv()


def store_kernel(
    group,
    att_hbm, gq_hbm, mine_hbm, recv_hbm, att_out, gq_out, gk_out, gv_out,
    att_ref, gq_ref, mine_ref, recv_ref, gk_ref, gv_ref, in_sem, out_sem,
):
    moves = ((mine_hbm, mine_ref), (recv_hbm, recv_ref), (att_hbm, att_ref), (gq_hbm, gq_ref))
    loads = [pltpu.make_async_copy(a, b, in_sem.at[n]) for n, (a, b) in enumerate(moves)]
    moves = ((att_ref, att_out), (gq_ref, gq_out), (gk_ref, gk_out), (gv_ref, gv_out))
    stores = [pltpu.make_async_copy(a, b, out_sem.at[n]) for n, (a, b) in enumerate(moves)]
    for load in loads:
        load.start()
    loads[0].wait()
    loads[1].wait()
    for part, out in ((0, gk_ref), (1, gv_ref)):
        total = mine_ref[part]
        for d in range(group - 1):
            total = total + recv_ref[part, d].astype(F32)
        out[...] = total.T.astype(BF16)
        stores[2 + part].start()
    for n in range(2):
        loads[2 + n].wait()
        stores[n].start()
    for store in stores:
        store.wait()


def solution(mesh):
    segments, group = mesh.shape["outer"], mesh.shape["inner"]

    def body(queries, key_vectors, value_vectors, grad_output, positions):
        tok, full = queries.shape
        dim = key_vectors.shape[1]
        heads = full // dim
        blocks, rows = 2 * group, heads * tok
        keys = blocks * tok
        wide, narrow = (tok, full), (tok, dim)
        scratch = [
            (wide, BF16),
            (wide, BF16),
            ((1, tok), jnp.int32),
            ((group, tok + 16, dim), BF16),
            ((group, tok, dim), BF16),
            ((group, tok, dim), BF16),
            ((group, tok, dim), BF16),
            ((rows, dim), BF16),
            ((rows, dim), BF16),
            ((dim, rows), BF16),
            ((dim, rows), BF16),
            ((rows, keys), F32),
            ((rows, keys), F32),
            ((rows, keys), BF16),
            ((2, group, dim, tok), BF16),
            ((2, group, dim, tok), BF16),
            ((2, group, dim, tok), BF16),
            ((2, dim, tok), F32),
            (wide, BF16),
            (wide, BF16),
            ((tok, tok), F32),
            ((rows, 1), F32),
            ((rows, 1), F32),
            ((rows, 1), F32),
        ]
        made = [(wide, BF16), (wide, BF16), ((2, dim, tok), F32), ((2, group - 1, dim, tok), BF16)]
        results = [(wide, BF16), (wide, BF16), (narrow, BF16), (narrow, BF16)]
        hbm = pl.BlockSpec(memory_space=pl.ANY)
        sem = pltpu.SemaphoreType.DMA
        partial = pl.pallas_call(
            functools.partial(kernel, segments, group, heads, dim, tok),
            out_shape=[jax.ShapeDtypeStruct(s, t) for s, t in made],
            in_specs=[hbm] * 5,
            out_specs=[hbm] * 4,
            scratch_shapes=[pltpu.VMEM(s, t) for s, t in scratch]
            + [sem((5,)), sem((4,))]
            + [sem((group,))] * 8
            + [sem((2, group))] * 4,
            compiler_params=pltpu.CompilerParams(
                collective_id=0, has_side_effects=True, vmem_limit_bytes=vmem_bytes
            ),
            name="window_attention",
        )(queries, key_vectors, value_vectors, grad_output, positions.reshape(1, tok))
        return pl.pallas_call(
            functools.partial(store_kernel, group),
            out_shape=[jax.ShapeDtypeStruct(s, t) for s, t in results],
            in_specs=[hbm] * 4,
            out_specs=[hbm] * 4,
            scratch_shapes=[pltpu.VMEM(s, t) for s, t in made + results[2:]] + [sem((4,))] * 2,
            compiler_params=pltpu.CompilerParams(vmem_limit_bytes=vmem_bytes),
            name="store_results",
        )(*partial)

    rows = P(("outer", "inner"), None)
    return jax.shard_map(
        body,
        mesh=mesh,
        in_specs=(rows, rows, rows, rows, P(("outer", "inner"))),
        out_specs=(rows, rows, rows, rows),
        check_vma=False,
    )
```

```python
import functools
import math

import jax
import jax.numpy as jnp
from jax import lax
from jax.experimental import pallas as pl
from jax.experimental.pallas import tpu as pltpu
from jax.sharding import PartitionSpec as P

masked_score = -1e30
vmem_bytes = (64 << 20) - (600 << 10)
MESH = pl.DeviceIdType.MESH
F32 = jnp.float32
BF16 = jnp.bfloat16


def dot_nt(a, b):
    return lax.dot_general(a, b, (((1,), (1,)), ((), ())), preferred_element_type=F32)


def dot_nn(a, b):
    return lax.dot_general(a, b, (((1,), (0,)), ((), ())), preferred_element_type=F32)


def kernel(
    segments, group, heads, dim, tok,
    q_hbm, k_hbm, v_hbm, do_hbm, pos_hbm,
    att_hbm, gq_hbm, mine_hbm, recv_hbm,
    q_ref, do_ref, pos_ref, k_own, v_own, k_prev, v_prev, qs, dos, q_t, do_t, s_ref, dp_ref, w_ref, ds_ref,
    p_send, p_recv, g_send, g_own, g_mine, att_ref, gq_ref,
    in_sem, out_sem, k_ssem, k_rsem, v_ssem, v_rsem, kf_ssem, kf_rsem, vf_ssem, vf_rsem,
    p_ssem, p_rsem, g_ssem, g_rsem,
):
    seg = lax.axis_index("outer")
    me = lax.axis_index("inner")
    nxt = lax.rem(seg + 1, segments)
    prv = lax.rem(seg + segments - 1, segments)
    scale = float(dim) ** -0.5
    blocks = 2 * group

    loads = [
        pltpu.make_async_copy(k_hbm, k_own.at[0, pl.ds(0, tok)], in_sem.at[0]),
        pltpu.make_async_copy(pos_hbm, pos_ref, in_sem.at[1]),
        pltpu.make_async_copy(v_hbm, v_own.at[0], in_sem.at[2]),
        pltpu.make_async_copy(q_hbm, q_ref, in_sem.at[3]),
        pltpu.make_async_copy(do_hbm, do_ref, in_sem.at[4]),
    ]
    stores = [
        pltpu.make_async_copy(att_ref, att_hbm, out_sem.at[0]),
        pltpu.make_async_copy(gq_ref, gq_hbm, out_sem.at[1]),
        pltpu.make_async_copy(g_mine.at[0], mine_hbm.at[0], out_sem.at[2]),
        pltpu.make_async_copy(g_mine.at[1], mine_hbm.at[1], out_sem.at[3]),
    ]
    for load in loads:
        load.start()

    barrier = pltpu.get_barrier_semaphore()
    partners = [(seg, lax.rem(me + d, group)) for d in range(1, group)] + [(nxt, me), (prv, me)]
    for partner in partners:
        pl.semaphore_signal(barrier, inc=1, device_id=partner, device_id_type=MESH)

    for load in loads[:3]:
        load.wait()
    pos = pos_ref[...]
    pos_hi = jnp.broadcast_to((pos >> 7).astype(F32), (8, tok))
    pos_lo = jnp.broadcast_to((pos & 127).astype(F32), (8, tok))
    k_own[0, tok:, :] = jnp.concatenate([pos_hi, pos_lo], axis=0).astype(BF16)
    pl.semaphore_wait(barrier, len(partners))

    def gather(buf, ssem, rsem, d):
        return pltpu.make_async_remote_copy(
            src_ref=buf.at[0], dst_ref=buf.at[d], send_sem=ssem.at[d], recv_sem=rsem.at[d],
            device_id=(seg, lax.rem(me + group - d, group)), device_id_type=MESH,
        )

    def forward(src, dst, ssem, rsem, d):
        return pltpu.make_async_remote_copy(
            src_ref=src.at[d, pl.ds(0, tok)], dst_ref=dst.at[d],
            send_sem=ssem.at[d], recv_sem=rsem.at[d],
            device_id=(nxt, me), device_id_type=MESH,
        )

    others = range(1, group)
    k_copies = {d: gather(k_own, k_ssem, k_rsem, d) for d in others}
    v_copies = {d: gather(v_own, v_ssem, v_rsem, d) for d in others}
    k_forwards = [forward(k_own, k_prev, kf_ssem, kf_rsem, d) for d in range(group)]
    v_forwards = [forward(v_own, v_prev, vf_ssem, vf_rsem, d) for d in range(group)]
    for d in others:
        k_copies[d].start()
    k_forwards[0].start()

    for load in loads[3:]:
        load.wait()
    for h in range(heads):
        rows, cols = slice(h * tok, (h + 1) * tok), slice(h * dim, (h + 1) * dim)
        q_h, do_h = q_ref[:, cols], do_ref[:, cols]
        qs[rows, :] = q_h
        dos[rows, :] = do_h
        q_t[:, rows] = q_h.astype(F32).T.astype(BF16)
        do_t[:, rows] = do_h.astype(F32).T.astype(BF16)
    for d in others:
        v_copies[d].start()
    v_forwards[0].start()

    pos_col = jnp.broadcast_to(pos.astype(F32), (tok, tok)).T
    prev_bias = jnp.where(seg > 0, 0.0, masked_score).astype(F32)

    def keys_of(block):
        return k_own[block, 0:tok, :] if block < group else k_prev[block - group]

    def values_of(block):
        return v_own[block] if block < group else v_prev[block - group]

    def bias_of(block):
        if block >= group:
            return jnp.broadcast_to(prev_bias, (tok, tok))
        coded = k_own[block, tok:, :].astype(F32)
        key_pos = coded[0:1, :] * 128.0 + coded[8:9, :]
        return jnp.where(key_pos <= pos_col, 0.0, masked_score)

    def cat(parts, axis):
        return parts[0] if len(parts) == 1 else jnp.concatenate(parts, axis=axis)

    def columns(step):
        return slice(step[0] * tok, (step[-1] + 1) * tok)

    def score_step(step):
        width = len(step) * tok
        score = dot_nt(qs[...], cat([keys_of(b) for b in step], 0))
        bias = cat([bias_of(b) for b in step], 1)
        score = score.reshape(heads, tok, width) + bias[None]
        s_ref[:, columns(step)] = score.reshape(heads * tok, width)

    def grad_step(step):
        dp_ref[:, columns(step)] = dot_nt(dos[...], cat([values_of(b) for b in step], 0))

    short = jnp.minimum(me, group - 1 - me)
    ahead = jnp.where(me < group // 2, 1, -1)
    nearest = []
    for n in others:
        both_ways = (n + 1) // 2 * (1 if n % 2 == 1 else -1)
        offset = jnp.where(n <= 2 * short, both_ways, (n - short) * ahead)
        nearest.append(lax.rem(offset + group, group))

    score_step([0])
    for d in nearest:
        gather(k_own, k_ssem, k_rsem, d).wait_recv()
        forward(k_own, k_prev, kf_ssem, kf_rsem, d).start()
    score_step([1])
    for d in range(2, group, 2):
        score_step([d, d + 1])

    rate = scale * math.log2(math.e)
    own, prev = slice(0, group * tok), slice(group * tok, blocks * tok)
    own_top, own_sum = [], []
    for h in range(heads):
        rows = slice(h * tok, (h + 1) * tok)
        s = s_ref[rows, own]
        top = jnp.max(s, axis=1, keepdims=True)
        e = jnp.exp2((s - top) * rate)
        s_ref[rows, own] = e
        own_top.append(top)
        own_sum.append(jnp.sum(e, axis=1, keepdims=True))

    for d in nearest:
        gather(v_own, v_ssem, v_rsem, d).wait_recv()
        forward(v_own, v_prev, vf_ssem, vf_rsem, d).start()
    for d in range(0, group, 2):
        grad_step([d, d + 1])
    own_delta = []
    for h in range(heads):
        rows = slice(h * tok, (h + 1) * tok)
        own_delta.append(jnp.sum(s_ref[rows, own] * dp_ref[rows, own], axis=1, keepdims=True))

    for d in range(0, group, 2):
        k_forwards[d].wait_recv()
        k_forwards[d + 1].wait_recv()
        score_step([group + d, group + d + 1])
    own_scale = []
    for h in range(heads):
        rows = slice(h * tok, (h + 1) * tok)
        s = s_ref[rows, prev]
        top = jnp.maximum(own_top[h], jnp.max(s, axis=1, keepdims=True))
        e = jnp.exp2((s - top) * rate)
        shrink = jnp.exp2((own_top[h] - top) * rate)
        inv = 1.0 / (own_sum[h] * shrink + jnp.sum(e, axis=1, keepdims=True))
        w_ref[rows, prev] = (e * inv).astype(BF16)
        own_scale.append(shrink * inv)

    def prev_copy(part, first):
        return pltpu.make_async_remote_copy(
            src_ref=p_send.at[part, pl.ds(first, 2)], dst_ref=p_recv.at[part, pl.ds(first, 2)],
            send_sem=p_ssem.at[part, first], recv_sem=p_rsem.at[part, first],
            device_id=(prv, me), device_id_type=MESH,
        )

    def grad_copy(part, d):
        return pltpu.make_async_remote_copy(
            src_ref=g_send.at[part, d], dst_ref=recv_hbm.at[part, d - 1],
            send_sem=g_ssem.at[part, d], recv_sem=g_rsem.at[part, d],
            device_id=(seg, lax.rem(me + d, group)), device_id_type=MESH,
        )

    firsts = list(range(0, group, 2))
    prev_copies = {(p, f): prev_copy(p, f) for p in range(2) for f in firsts}
    grad_copies = {(p, d): grad_copy(p, d) for p in range(2) for d in others}

    def pair(first):
        return columns([first, first + 1])

    def send_prev(part, first, total):
        for n in range(2):
            p_send[part, first + n] = total[:, n * tok : (n + 1) * tok].astype(BF16)
        prev_copies[part, first].start()

    def send_own(part):
        for first in firsts[::-1]:
            prev_copies[part, first].wait_recv()
            for d in (first + 1, first):
                block = g_own[part, d] + p_recv[part, d].astype(F32)
                if d == 0:
                    g_mine[part] = block
                    stores[2 + part].start()
                else:
                    g_send[part, d] = block.astype(BF16)
                    grad_copies[part, d].start()

    def keep_own(part, first, total):
        for n in range(2):
            g_own[part, first + n] = total[:, n * tok : (n + 1) * tok]

    def key_terms(first):
        cols = pair(first)
        ds = (w_ref[:, cols].astype(F32) * (dp_ref[:, cols] - delta)).astype(BF16)
        ds_ref[:, cols] = ds
        return dot_nn(q_t[...], ds) * scale

    for first in firsts:
        send_prev(1, first, dot_nn(do_t[...], w_ref[:, pair(group + first)]))

    for h in range(heads):
        rows = slice(h * tok, (h + 1) * tok)
        w_ref[rows, own] = (s_ref[rows, own] * own_scale[h]).astype(BF16)
    for d in range(0, group, 2):
        v_forwards[d].wait_recv()
        v_forwards[d + 1].wait_recv()
        grad_step([group + d, group + d + 1])
    deltas = []
    for h in range(heads):
        rows = slice(h * tok, (h + 1) * tok)
        part = jnp.sum(w_ref[rows, prev].astype(F32) * dp_ref[rows, prev], axis=1, keepdims=True)
        deltas.append(own_delta[h] * own_scale[h] + part)
    delta = jnp.concatenate(deltas, axis=0)

    for first in firsts:
        send_prev(0, first, key_terms(group + first))
    for first in firsts:
        keep_own(1, first, dot_nn(do_t[...], w_ref[:, pair(first)]))
    send_own(1)
    for first in firsts:
        keep_own(0, first, key_terms(first))
    all_values = cat([values_of(b) for b in range(blocks)], 0)
    attended = dot_nn(w_ref[...], all_values).astype(BF16)
    for h in range(heads):
        att_ref[:, h * dim : (h + 1) * dim] = attended[h * tok : (h + 1) * tok]
    stores[0].start()
    send_own(0)

    all_keys = cat([keys_of(b) for b in range(blocks)], 0)
    gq = (dot_nn(ds_ref[...], all_keys) * scale).astype(BF16)
    for h in range(heads):
        gq_ref[:, h * dim : (h + 1) * dim] = gq[h * tok : (h + 1) * tok]
    stores[1].start()

    for copy in list(k_copies.values()) + list(v_copies.values()) + k_forwards + v_forwards:
        copy.wait_send()
    for copy in list(prev_copies.values()) + list(grad_copies.values()):
        copy.wait_send()
    for store in stores:
        store.wait()
    for copy in grad_copies.values():
        copy.wait_recv()


def store_kernel(
    group,
    att_hbm, gq_hbm, mine_hbm, recv_hbm, att_out, gq_out, gk_out, gv_out,
    att_ref, gq_ref, mine_ref, recv_ref, gk_ref, gv_ref, in_sem, out_sem,
):
    moves = ((mine_hbm, mine_ref), (recv_hbm, recv_ref), (att_hbm, att_ref), (gq_hbm, gq_ref))
    loads = [pltpu.make_async_copy(a, b, in_sem.at[n]) for n, (a, b) in enumerate(moves)]
    moves = ((att_ref, att_out), (gq_ref, gq_out), (gk_ref, gk_out), (gv_ref, gv_out))
    stores = [pltpu.make_async_copy(a, b, out_sem.at[n]) for n, (a, b) in enumerate(moves)]
    for load in loads:
        load.start()
    loads[0].wait()
    loads[1].wait()
    for part, out in ((0, gk_ref), (1, gv_ref)):
        total = mine_ref[part]
        for d in range(group - 1):
            total = total + recv_ref[part, d].astype(F32)
        out[...] = total.T.astype(BF16)
        stores[2 + part].start()
    for n in range(2):
        loads[2 + n].wait()
        stores[n].start()
    for store in stores:
        store.wait()


def solution(mesh):
    segments, group = mesh.shape["outer"], mesh.shape["inner"]

    def body(queries, key_vectors, value_vectors, grad_output, positions):
        tok, full = queries.shape
        dim = key_vectors.shape[1]
        heads = full // dim
        blocks, rows = 2 * group, heads * tok
        keys = blocks * tok
        wide, narrow = (tok, full), (tok, dim)
        scratch = [
            (wide, BF16),
            (wide, BF16),
            ((1, tok), jnp.int32),
            ((group, tok + 16, dim), BF16),
            ((group, tok, dim), BF16),
            ((group, tok, dim), BF16),
            ((group, tok, dim), BF16),
            ((rows, dim), BF16),
            ((rows, dim), BF16),
            ((dim, rows), BF16),
            ((dim, rows), BF16),
            ((rows, keys), F32),
            ((rows, keys), F32),
            ((rows, keys), BF16),
            ((rows, keys), BF16),
            ((2, group, dim, tok), BF16),
            ((2, group, dim, tok), BF16),
            ((2, group, dim, tok), BF16),
            ((2, group, dim, tok), F32),
            ((2, dim, tok), F32),
            (wide, BF16),
            (wide, BF16),
        ]
        made = [(wide, BF16), (wide, BF16), ((2, dim, tok), F32), ((2, group - 1, dim, tok), BF16)]
        results = [(wide, BF16), (wide, BF16), (narrow, BF16), (narrow, BF16)]
        hbm = pl.BlockSpec(memory_space=pl.ANY)
        sem = pltpu.SemaphoreType.DMA
        partial = pl.pallas_call(
            functools.partial(kernel, segments, group, heads, dim, tok),
            out_shape=[jax.ShapeDtypeStruct(s, t) for s, t in made],
            in_specs=[hbm] * 5,
            out_specs=[hbm] * 4,
            scratch_shapes=[pltpu.VMEM(s, t) for s, t in scratch]
            + [sem((5,)), sem((4,))]
            + [sem((group,))] * 8
            + [sem((2, group))] * 4,
            compiler_params=pltpu.CompilerParams(
                collective_id=0, has_side_effects=True, vmem_limit_bytes=vmem_bytes
            ),
            name="window_attention",
        )(queries, key_vectors, value_vectors, grad_output, positions.reshape(1, tok))
        return pl.pallas_call(
            functools.partial(store_kernel, group),
            out_shape=[jax.ShapeDtypeStruct(s, t) for s, t in results],
            in_specs=[hbm] * 4,
            out_specs=[hbm] * 4,
            scratch_shapes=[pltpu.VMEM(s, t) for s, t in made + results[2:]] + [sem((4,))] * 2,
            compiler_params=pltpu.CompilerParams(vmem_limit_bytes=vmem_bytes),
            name="store_results",
        )(*partial)

    rows = P(("outer", "inner"), None)
    return jax.shard_map(
        body,
        mesh=mesh,
        in_specs=(rows, rows, rows, rows, P(("outer", "inner"))),
        out_specs=(rows, rows, rows, rows),
        check_vma=False,
    )
```

```python
import functools
import math

import jax
import jax.numpy as jnp
from jax import lax
from jax.experimental import pallas as pl
from jax.experimental.pallas import tpu as pltpu
from jax.sharding import PartitionSpec as P

masked_score = -1e30
vmem_bytes = (64 << 20) - (600 << 10)
MESH = pl.DeviceIdType.MESH
F32 = jnp.float32
BF16 = jnp.bfloat16


def dot_nt(a, b):
    return lax.dot_general(a, b, (((1,), (1,)), ((), ())), preferred_element_type=F32)


def dot_nn(a, b):
    return lax.dot_general(a, b, (((1,), (0,)), ((), ())), preferred_element_type=F32)


def kernel(
    segments, group, heads, dim, tok,
    q_hbm, k_hbm, v_hbm, do_hbm, pos_hbm,
    att_hbm, gq_hbm, mine_hbm, recv_hbm,
    q_ref, do_ref, pos_ref, k_own, v_own, k_prev, v_prev, qs, dos, q_t, do_t, s_ref, dp_ref, w_ref, ds_ref,
    p_send, p_recv, g_send, g_own, g_mine, att_ref, gq_ref,
    in_sem, out_sem, k_ssem, k_rsem, v_ssem, v_rsem, kf_ssem, kf_rsem, vf_ssem, vf_rsem,
    p_ssem, p_rsem, g_ssem, g_rsem,
):
    seg = lax.axis_index("outer")
    me = lax.axis_index("inner")
    nxt = lax.rem(seg + 1, segments)
    prv = lax.rem(seg + segments - 1, segments)
    scale = float(dim) ** -0.5
    blocks = 2 * group

    loads = [
        pltpu.make_async_copy(k_hbm, k_own.at[0, pl.ds(0, tok)], in_sem.at[0]),
        pltpu.make_async_copy(pos_hbm, pos_ref, in_sem.at[1]),
        pltpu.make_async_copy(v_hbm, v_own.at[0], in_sem.at[2]),
        pltpu.make_async_copy(q_hbm, q_ref, in_sem.at[3]),
        pltpu.make_async_copy(do_hbm, do_ref, in_sem.at[4]),
    ]
    stores = [
        pltpu.make_async_copy(att_ref, att_hbm, out_sem.at[0]),
        pltpu.make_async_copy(gq_ref, gq_hbm, out_sem.at[1]),
        pltpu.make_async_copy(g_mine.at[0], mine_hbm.at[0], out_sem.at[2]),
        pltpu.make_async_copy(g_mine.at[1], mine_hbm.at[1], out_sem.at[3]),
    ]
    for load in loads:
        load.start()

    barrier = pltpu.get_barrier_semaphore()
    partners = [(seg, lax.rem(me + d, group)) for d in range(1, group)] + [(nxt, me), (prv, me)]
    for partner in partners:
        pl.semaphore_signal(barrier, inc=1, device_id=partner, device_id_type=MESH)

    for load in loads[:3]:
        load.wait()
    pos = pos_ref[...]
    pos_hi = jnp.broadcast_to((pos >> 7).astype(F32), (8, tok))
    pos_lo = jnp.broadcast_to((pos & 127).astype(F32), (8, tok))
    k_own[0, tok:, :] = jnp.concatenate([pos_hi, pos_lo], axis=0).astype(BF16)
    pl.semaphore_wait(barrier, len(partners))

    def gather(buf, ssem, rsem, d):
        return pltpu.make_async_remote_copy(
            src_ref=buf.at[0], dst_ref=buf.at[d], send_sem=ssem.at[d], recv_sem=rsem.at[d],
            device_id=(seg, lax.rem(me + group - d, group)), device_id_type=MESH,
        )

    def forward(src, dst, ssem, rsem, d):
        return pltpu.make_async_remote_copy(
            src_ref=src.at[d, pl.ds(0, tok)], dst_ref=dst.at[d],
            send_sem=ssem.at[d], recv_sem=rsem.at[d],
            device_id=(nxt, me), device_id_type=MESH,
        )

    others = range(1, group)
    k_copies = {d: gather(k_own, k_ssem, k_rsem, d) for d in others}
    v_copies = {d: gather(v_own, v_ssem, v_rsem, d) for d in others}
    k_forwards = [forward(k_own, k_prev, kf_ssem, kf_rsem, d) for d in range(group)]
    v_forwards = [forward(v_own, v_prev, vf_ssem, vf_rsem, d) for d in range(group)]
    for d in others:
        k_copies[d].start()
    k_forwards[0].start()

    for load in loads[3:]:
        load.wait()
    for h in range(heads):
        rows, cols = slice(h * tok, (h + 1) * tok), slice(h * dim, (h + 1) * dim)
        q_h, do_h = q_ref[:, cols], do_ref[:, cols]
        qs[rows, :] = q_h
        dos[rows, :] = do_h
        q_t[:, rows] = q_h.astype(F32).T.astype(BF16)
        do_t[:, rows] = do_h.astype(F32).T.astype(BF16)
    for d in others:
        v_copies[d].start()
    v_forwards[0].start()

    pos_col = jnp.broadcast_to(pos.astype(F32), (tok, tok)).T
    prev_bias = jnp.where(seg > 0, 0.0, masked_score).astype(F32)

    def keys_of(block):
        return k_own[block, 0:tok, :] if block < group else k_prev[block - group]

    def values_of(block):
        return v_own[block] if block < group else v_prev[block - group]

    def bias_of(block):
        if block >= group:
            return jnp.broadcast_to(prev_bias, (tok, tok))
        coded = k_own[block, tok:, :].astype(F32)
        key_pos = coded[0:1, :] * 128.0 + coded[8:9, :]
        return jnp.where(key_pos <= pos_col, 0.0, masked_score)

    def cat(parts, axis):
        return parts[0] if len(parts) == 1 else jnp.concatenate(parts, axis=axis)

    def columns(step):
        return slice(step[0] * tok, (step[-1] + 1) * tok)

    def score_step(step):
        width = len(step) * tok
        score = dot_nt(qs[...], cat([keys_of(b) for b in step], 0))
        bias = cat([bias_of(b) for b in step], 1)
        score = score.reshape(heads, tok, width) + bias[None]
        s_ref[:, columns(step)] = score.reshape(heads * tok, width)

    def grad_step(step):
        dp_ref[:, columns(step)] = dot_nt(dos[...], cat([values_of(b) for b in step], 0))

    short = jnp.minimum(me, group - 1 - me)
    ahead = jnp.where(me < group // 2, 1, -1)
    nearest = []
    for n in others:
        both_ways = (n + 1) // 2 * (1 if n % 2 == 1 else -1)
        offset = jnp.where(n <= 2 * short, both_ways, (n - short) * ahead)
        nearest.append(lax.rem(offset + group, group))

    score_step([0])
    for d in nearest:
        gather(k_own, k_ssem, k_rsem, d).wait_recv()
        forward(k_own, k_prev, kf_ssem, kf_rsem, d).start()
    score_step([1])
    for d in range(2, group, 2):
        score_step([d, d + 1])

    rate = scale * math.log2(math.e)
    own, prev = slice(0, group * tok), slice(group * tok, blocks * tok)
    last = heads // 2 - 1
    chunks = [slice(n * 2 * tok, (n + 1) * 2 * tok) for n in range(heads // 2)]
    own_top, own_sum = [], []
    for rows in chunks:
        s = s_ref[rows, own]
        top = jnp.max(s, axis=1, keepdims=True)
        e = jnp.exp2((s - top) * rate)
        s_ref[rows, own] = e
        own_top.append(top)
        own_sum.append(jnp.sum(e, axis=1, keepdims=True))

    for d in nearest:
        gather(v_own, v_ssem, v_rsem, d).wait_recv()
        forward(v_own, v_prev, vf_ssem, vf_rsem, d).start()
    for d in range(0, group, 2):
        grad_step([d, d + 1])
    own_delta = []
    for rows in chunks:
        own_delta.append(jnp.sum(s_ref[rows, own] * dp_ref[rows, own], axis=1, keepdims=True))

    def prev_copy(part, first):
        return pltpu.make_async_remote_copy(
            src_ref=p_send.at[part, pl.ds(first, 2)], dst_ref=p_recv.at[part, pl.ds(first, 2)],
            send_sem=p_ssem.at[part, first], recv_sem=p_rsem.at[part, first],
            device_id=(prv, me), device_id_type=MESH,
        )

    def grad_copy(part, d):
        return pltpu.make_async_remote_copy(
            src_ref=g_send.at[part, d], dst_ref=recv_hbm.at[part, d - 1],
            send_sem=g_ssem.at[part, d], recv_sem=g_rsem.at[part, d],
            device_id=(seg, lax.rem(me + d, group)), device_id_type=MESH,
        )

    firsts = list(range(0, group, 2))
    prev_copies = {(p, f): prev_copy(p, f) for p in range(2) for f in firsts}
    grad_copies = {(p, d): grad_copy(p, d) for p in range(2) for d in others}

    def pair(first):
        return columns([first, first + 1])

    def send_prev(part, total):
        for first in firsts:
            for d in (first, first + 1):
                p_send[part, d] = total[:, d * tok : (d + 1) * tok].astype(BF16)
            prev_copies[part, first].start()

    def send_own(part):
        for first in firsts[::-1]:
            prev_copies[part, first].wait_recv()
            for d in (first + 1, first):
                block = g_own[part, d] + p_recv[part, d].astype(F32)
                if d == 0:
                    g_mine[part] = block
                    stores[2 + part].start()
                else:
                    g_send[part, d] = block.astype(BF16)
                    grad_copies[part, d].start()

    def keep_own(part, first, total):
        for n in range(2):
            g_own[part, first + n] = total[:, n * tok : (n + 1) * tok]

    def key_terms(first):
        cols = pair(first)
        ds = (w_ref[:, cols].astype(F32) * (dp_ref[:, cols] - delta)).astype(BF16)
        ds_ref[:, cols] = ds
        return dot_nn(q_t[...], ds) * scale

    for copy in k_forwards:
        copy.wait_recv()
    prev_keys = cat([keys_of(group + d) for d in range(group)], 0)
    own_scale, total = [], None
    ready = dot_nt(qs[chunks[0], :], prev_keys)
    for n, rows in enumerate(chunks):
        s = ready + prev_bias
        if n < last:
            ready = dot_nt(qs[chunks[n + 1], :], prev_keys)
        top = jnp.maximum(own_top[n], jnp.max(s, axis=1, keepdims=True))
        e = jnp.exp2((s - top) * rate)
        shrink = jnp.exp2((own_top[n] - top) * rate)
        inv = 1.0 / (own_sum[n] * shrink + jnp.sum(e, axis=1, keepdims=True))
        w = (e * inv).astype(BF16)
        w_ref[rows, prev] = w
        own_scale.append(shrink * inv)
        term = dot_nn(do_t[:, rows], w)
        total = term if total is None else total + term
    send_prev(1, total)

    for n, rows in enumerate(chunks):
        w_ref[rows, own] = (s_ref[rows, own] * own_scale[n]).astype(BF16)
    for copy in v_forwards:
        copy.wait_recv()
    prev_values = cat([values_of(group + d) for d in range(group)], 0)
    deltas, total = [], None
    ready = dot_nt(dos[chunks[0], :], prev_values)
    for n, rows in enumerate(chunks):
        dp = ready
        if n < last:
            ready = dot_nt(dos[chunks[n + 1], :], prev_values)
        w = w_ref[rows, prev].astype(F32)
        row_delta = own_delta[n] * own_scale[n] + jnp.sum(w * dp, axis=1, keepdims=True)
        deltas.append(row_delta)
        ds = (w * (dp - row_delta)).astype(BF16)
        ds_ref[rows, prev] = ds
        term = dot_nn(q_t[:, rows], ds)
        total = term if total is None else total + term
    send_prev(0, total * scale)
    delta = jnp.concatenate(deltas, axis=0)

    for first in firsts:
        keep_own(1, first, dot_nn(do_t[...], w_ref[:, pair(first)]))
    send_own(1)
    for first in firsts:
        keep_own(0, first, key_terms(first))
    all_values = cat([values_of(b) for b in range(blocks)], 0)
    attended = dot_nn(w_ref[...], all_values).astype(BF16)
    for h in range(heads):
        att_ref[:, h * dim : (h + 1) * dim] = attended[h * tok : (h + 1) * tok]
    stores[0].start()
    send_own(0)

    all_keys = cat([keys_of(b) for b in range(blocks)], 0)
    gq = (dot_nn(ds_ref[...], all_keys) * scale).astype(BF16)
    for h in range(heads):
        gq_ref[:, h * dim : (h + 1) * dim] = gq[h * tok : (h + 1) * tok]
    stores[1].start()

    for copy in list(k_copies.values()) + list(v_copies.values()) + k_forwards + v_forwards:
        copy.wait_send()
    for copy in list(prev_copies.values()) + list(grad_copies.values()):
        copy.wait_send()
    for store in stores:
        store.wait()
    for copy in grad_copies.values():
        copy.wait_recv()


def store_kernel(
    group,
    att_hbm, gq_hbm, mine_hbm, recv_hbm, att_out, gq_out, gk_out, gv_out,
    att_ref, gq_ref, mine_ref, recv_ref, gk_ref, gv_ref, in_sem, out_sem,
):
    moves = ((mine_hbm, mine_ref), (recv_hbm, recv_ref), (att_hbm, att_ref), (gq_hbm, gq_ref))
    loads = [pltpu.make_async_copy(a, b, in_sem.at[n]) for n, (a, b) in enumerate(moves)]
    moves = ((att_ref, att_out), (gq_ref, gq_out), (gk_ref, gk_out), (gv_ref, gv_out))
    stores = [pltpu.make_async_copy(a, b, out_sem.at[n]) for n, (a, b) in enumerate(moves)]
    for load in loads:
        load.start()
    loads[0].wait()
    loads[1].wait()
    for part, out in ((0, gk_ref), (1, gv_ref)):
        total = mine_ref[part]
        for d in range(group - 1):
            total = total + recv_ref[part, d].astype(F32)
        out[...] = total.T.astype(BF16)
        stores[2 + part].start()
    for n in range(2):
        loads[2 + n].wait()
        stores[n].start()
    for store in stores:
        store.wait()


def solution(mesh):
    segments, group = mesh.shape["outer"], mesh.shape["inner"]

    def body(queries, key_vectors, value_vectors, grad_output, positions):
        tok, full = queries.shape
        dim = key_vectors.shape[1]
        heads = full // dim
        blocks, rows = 2 * group, heads * tok
        keys = blocks * tok
        wide, narrow = (tok, full), (tok, dim)
        scratch = [
            (wide, BF16),
            (wide, BF16),
            ((1, tok), jnp.int32),
            ((group, tok + 16, dim), BF16),
            ((group, tok, dim), BF16),
            ((group, tok, dim), BF16),
            ((group, tok, dim), BF16),
            ((rows, dim), BF16),
            ((rows, dim), BF16),
            ((dim, rows), BF16),
            ((dim, rows), BF16),
            ((rows, group * tok), F32),
            ((rows, group * tok), F32),
            ((rows, keys), BF16),
            ((rows, keys), BF16),
            ((2, group, dim, tok), BF16),
            ((2, group, dim, tok), BF16),
            ((2, group, dim, tok), BF16),
            ((2, group, dim, tok), F32),
            ((2, dim, tok), F32),
            (wide, BF16),
            (wide, BF16),
        ]
        made = [(wide, BF16), (wide, BF16), ((2, dim, tok), F32), ((2, group - 1, dim, tok), BF16)]
        results = [(wide, BF16), (wide, BF16), (narrow, BF16), (narrow, BF16)]
        hbm = pl.BlockSpec(memory_space=pl.ANY)
        sem = pltpu.SemaphoreType.DMA
        partial = pl.pallas_call(
            functools.partial(kernel, segments, group, heads, dim, tok),
            out_shape=[jax.ShapeDtypeStruct(s, t) for s, t in made],
            in_specs=[hbm] * 5,
            out_specs=[hbm] * 4,
            scratch_shapes=[pltpu.VMEM(s, t) for s, t in scratch]
            + [sem((5,)), sem((4,))]
            + [sem((group,))] * 8
            + [sem((2, group))] * 4,
            compiler_params=pltpu.CompilerParams(
                collective_id=0, has_side_effects=True, vmem_limit_bytes=vmem_bytes
            ),
            name="window_attention",
        )(queries, key_vectors, value_vectors, grad_output, positions.reshape(1, tok))
        return pl.pallas_call(
            functools.partial(store_kernel, group),
            out_shape=[jax.ShapeDtypeStruct(s, t) for s, t in results],
            in_specs=[hbm] * 4,
            out_specs=[hbm] * 4,
            scratch_shapes=[pltpu.VMEM(s, t) for s, t in made + results[2:]] + [sem((4,))] * 2,
            compiler_params=pltpu.CompilerParams(vmem_limit_bytes=vmem_bytes),
            name="store_results",
        )(*partial)

    rows = P(("outer", "inner"), None)
    return jax.shard_map(
        body,
        mesh=mesh,
        in_specs=(rows, rows, rows, rows, P(("outer", "inner"))),
        out_specs=(rows, rows, rows, rows),
        check_vma=False,
    )
```

```python
import functools
import math

import jax
import jax.numpy as jnp
from jax import lax
from jax.experimental import pallas as pl
from jax.experimental.pallas import tpu as pltpu
from jax.sharding import PartitionSpec as P

masked_score = -1e30
vmem_bytes = (64 << 20) - (600 << 10)
MESH = pl.DeviceIdType.MESH
F32 = jnp.float32
BF16 = jnp.bfloat16


def dot_nt(a, b):
    return lax.dot_general(a, b, (((1,), (1,)), ((), ())), preferred_element_type=F32)


def dot_nn(a, b):
    return lax.dot_general(a, b, (((1,), (0,)), ((), ())), preferred_element_type=F32)


def kernel(
    segments, group, heads, dim, tok,
    q_hbm, k_hbm, v_hbm, do_hbm, pos_hbm,
    att_hbm, gq_hbm, mine_hbm, recv_hbm,
    q_ref, do_ref, pos_ref, k_own, v_own, k_prev, v_prev, qs, dos, q_t, do_t, s_ref, dp_ref, w_ref, ds_ref,
    p_send, p_recv, g_send, g_own, g_mine, att_ref, gq_ref,
    in_sem, out_sem, k_ssem, k_rsem, v_ssem, v_rsem, kf_ssem, kf_rsem, vf_ssem, vf_rsem,
    p_ssem, p_rsem, g_ssem, g_rsem,
):
    seg = lax.axis_index("outer")
    me = lax.axis_index("inner")
    nxt = lax.rem(seg + 1, segments)
    prv = lax.rem(seg + segments - 1, segments)
    scale = float(dim) ** -0.5
    blocks = 2 * group

    loads = [
        pltpu.make_async_copy(k_hbm, k_own.at[0, pl.ds(0, tok)], in_sem.at[0]),
        pltpu.make_async_copy(pos_hbm, pos_ref, in_sem.at[1]),
        pltpu.make_async_copy(v_hbm, v_own.at[0], in_sem.at[2]),
        pltpu.make_async_copy(q_hbm, q_ref, in_sem.at[3]),
        pltpu.make_async_copy(do_hbm, do_ref, in_sem.at[4]),
    ]
    stores = [
        pltpu.make_async_copy(att_ref, att_hbm, out_sem.at[0]),
        pltpu.make_async_copy(gq_ref, gq_hbm, out_sem.at[1]),
        pltpu.make_async_copy(g_mine.at[0], mine_hbm.at[0], out_sem.at[2]),
        pltpu.make_async_copy(g_mine.at[1], mine_hbm.at[1], out_sem.at[3]),
    ]
    barrier = pltpu.get_barrier_semaphore()
    partners = [(seg, lax.rem(me + d, group)) for d in range(1, group)] + [(nxt, me), (prv, me)]
    for partner in partners:
        pl.semaphore_signal(barrier, inc=1, device_id=partner, device_id_type=MESH)
    for load in loads:
        load.start()

    for load in loads[:3]:
        load.wait()
    pos = pos_ref[...]
    pos_hi = jnp.broadcast_to((pos >> 7).astype(F32), (8, tok))
    pos_lo = jnp.broadcast_to((pos & 127).astype(F32), (8, tok))
    k_own[0, tok:, :] = jnp.concatenate([pos_hi, pos_lo], axis=0).astype(BF16)
    pl.semaphore_wait(barrier, len(partners))

    def gather(buf, ssem, rsem, d):
        return pltpu.make_async_remote_copy(
            src_ref=buf.at[0], dst_ref=buf.at[d], send_sem=ssem.at[d], recv_sem=rsem.at[d],
            device_id=(seg, lax.rem(me + group - d, group)), device_id_type=MESH,
        )

    def forward(src, dst, ssem, rsem, d):
        return pltpu.make_async_remote_copy(
            src_ref=src.at[d, pl.ds(0, tok)], dst_ref=dst.at[d],
            send_sem=ssem.at[d], recv_sem=rsem.at[d],
            device_id=(nxt, me), device_id_type=MESH,
        )

    others = range(1, group)
    k_copies = {d: gather(k_own, k_ssem, k_rsem, d) for d in others}
    v_copies = {d: gather(v_own, v_ssem, v_rsem, d) for d in others}
    k_forwards = [forward(k_own, k_prev, kf_ssem, kf_rsem, d) for d in range(group)]
    v_forwards = [forward(v_own, v_prev, vf_ssem, vf_rsem, d) for d in range(group)]
    for d in others:
        k_copies[d].start()
    k_forwards[0].start()

    for load in loads[3:]:
        load.wait()
    for h in range(heads):
        rows, cols = slice(h * tok, (h + 1) * tok), slice(h * dim, (h + 1) * dim)
        q_h, do_h = q_ref[:, cols], do_ref[:, cols]
        qs[rows, :] = q_h
        dos[rows, :] = do_h
        q_t[:, rows] = q_h.astype(F32).T.astype(BF16)
        do_t[:, rows] = do_h.astype(F32).T.astype(BF16)
    v_forwards[0].start()

    pos_col = jnp.broadcast_to(pos.astype(F32), (tok, tok)).T
    prev_bias = jnp.where(seg > 0, 0.0, masked_score).astype(F32)

    def keys_of(block):
        return k_own[block, 0:tok, :] if block < group else k_prev[block - group]

    def values_of(block):
        return v_own[block] if block < group else v_prev[block - group]

    def bias_of(block):
        if block >= group:
            return jnp.broadcast_to(prev_bias, (tok, tok))
        coded = k_own[block, tok:, :].astype(F32)
        key_pos = coded[0:1, :] * 128.0 + coded[8:9, :]
        return jnp.where(key_pos <= pos_col, 0.0, masked_score)

    def cat(parts, axis):
        return parts[0] if len(parts) == 1 else jnp.concatenate(parts, axis=axis)

    def columns(step):
        return slice(step[0] * tok, (step[-1] + 1) * tok)

    def score_step(step):
        width = len(step) * tok
        score = dot_nt(qs[...], cat([keys_of(b) for b in step], 0))
        bias = cat([bias_of(b) for b in step], 1)
        score = score.reshape(heads, tok, width) + bias[None]
        s_ref[:, columns(step)] = score.reshape(heads * tok, width)

    def grad_step(step):
        dp_ref[:, columns(step)] = dot_nt(dos[...], cat([values_of(b) for b in step], 0))

    short = jnp.minimum(me, group - 1 - me)
    ahead = jnp.where(me < group // 2, 1, -1)
    nearest = []
    for n in others:
        both_ways = (n + 1) // 2 * (1 if n % 2 == 1 else -1)
        offset = jnp.where(n <= 2 * short, both_ways, (n - short) * ahead)
        nearest.append(lax.rem(offset + group, group))

    score_step([0])
    for d in nearest:
        gather(k_own, k_ssem, k_rsem, d).wait_recv()
        forward(k_own, k_prev, kf_ssem, kf_rsem, d).start()
    for d in others:
        v_copies[d].start()
    score_step([1])
    for d in range(2, group, 2):
        score_step([d, d + 1])

    rate = scale * math.log2(math.e)
    own, prev = slice(0, group * tok), slice(group * tok, blocks * tok)
    last = heads // 2 - 1
    chunks = [slice(n * 2 * tok, (n + 1) * 2 * tok) for n in range(heads // 2)]
    own_top, own_sum = [], []
    for rows in chunks:
        s = s_ref[rows, own]
        top = jnp.max(s, axis=1, keepdims=True)
        e = jnp.exp2((s - top) * rate)
        s_ref[rows, own] = e
        own_top.append(top)
        own_sum.append(jnp.sum(e, axis=1, keepdims=True))

    for d in nearest:
        gather(v_own, v_ssem, v_rsem, d).wait_recv()
        forward(v_own, v_prev, vf_ssem, vf_rsem, d).start()
    for d in range(0, group, 2):
        grad_step([d, d + 1])
    own_delta = []
    for rows in chunks:
        own_delta.append(jnp.sum(s_ref[rows, own] * dp_ref[rows, own], axis=1, keepdims=True))

    def prev_copy(part, first):
        return pltpu.make_async_remote_copy(
            src_ref=p_send.at[part, pl.ds(first, 2)], dst_ref=p_recv.at[part, pl.ds(first, 2)],
            send_sem=p_ssem.at[part, first], recv_sem=p_rsem.at[part, first],
            device_id=(prv, me), device_id_type=MESH,
        )

    def grad_copy(part, d):
        return pltpu.make_async_remote_copy(
            src_ref=g_send.at[part, d], dst_ref=recv_hbm.at[part, d - 1],
            send_sem=g_ssem.at[part, d], recv_sem=g_rsem.at[part, d],
            device_id=(seg, lax.rem(me + d, group)), device_id_type=MESH,
        )

    firsts = list(range(0, group, 2))
    prev_copies = {(p, f): prev_copy(p, f) for p in range(2) for f in firsts}
    grad_copies = {(p, d): grad_copy(p, d) for p in range(2) for d in others}

    def pair(first):
        return columns([first, first + 1])

    def send_prev(part, total):
        for first in firsts:
            for d in (first, first + 1):
                p_send[part, d] = total[:, d * tok : (d + 1) * tok].astype(BF16)
            prev_copies[part, first].start()

    def send_own(part):
        for first in firsts[::-1]:
            prev_copies[part, first].wait_recv()
            for d in (first + 1, first):
                block = g_own[part, d] + p_recv[part, d].astype(F32)
                if d == 0:
                    g_mine[part] = block
                    stores[2 + part].start()
                else:
                    g_send[part, d] = block.astype(BF16)
                    grad_copies[part, d].start()

    def keep_own(part, first, total):
        for n in range(2):
            g_own[part, first + n] = total[:, n * tok : (n + 1) * tok]

    def key_terms(first):
        cols = pair(first)
        ds = (w_ref[:, cols].astype(F32) * (dp_ref[:, cols] - delta)).astype(BF16)
        ds_ref[:, cols] = ds
        return dot_nn(q_t[...], ds) * scale

    for copy in k_forwards:
        copy.wait_recv()
    prev_keys = cat([keys_of(group + d) for d in range(group)], 0)
    own_scale, total = [], None
    ready = dot_nt(qs[chunks[0], :], prev_keys)
    for n, rows in enumerate(chunks):
        s = ready + prev_bias
        if n < last:
            ready = dot_nt(qs[chunks[n + 1], :], prev_keys)
        top = jnp.maximum(own_top[n], jnp.max(s, axis=1, keepdims=True))
        e = jnp.exp2((s - top) * rate)
        shrink = jnp.exp2((own_top[n] - top) * rate)
        inv = 1.0 / (own_sum[n] * shrink + jnp.sum(e, axis=1, keepdims=True))
        w = (e * inv).astype(BF16)
        w_ref[rows, prev] = w
        own_scale.append(shrink * inv)
        term = dot_nn(do_t[:, rows], w)
        total = term if total is None else total + term
    send_prev(1, total)

    for n, rows in enumerate(chunks):
        w_ref[rows, own] = (s_ref[rows, own] * own_scale[n]).astype(BF16)
    for first in firsts:
        keep_own(1, first, dot_nn(do_t[...], w_ref[:, pair(first)]))
    for copy in v_forwards:
        copy.wait_recv()
    prev_values = cat([values_of(group + d) for d in range(group)], 0)
    deltas, total = [], None
    ready = dot_nt(dos[chunks[0], :], prev_values)
    for n, rows in enumerate(chunks):
        dp = ready
        if n < last:
            ready = dot_nt(dos[chunks[n + 1], :], prev_values)
        w = w_ref[rows, prev].astype(F32)
        row_delta = own_delta[n] * own_scale[n] + jnp.sum(w * dp, axis=1, keepdims=True)
        deltas.append(row_delta)
        ds = (w * (dp - row_delta)).astype(BF16)
        ds_ref[rows, prev] = ds
        term = dot_nn(q_t[:, rows], ds)
        total = term if total is None else total + term
    send_prev(0, total * scale)
    delta = jnp.concatenate(deltas, axis=0)

    send_own(1)
    for first in firsts:
        keep_own(0, first, key_terms(first))
    all_values = cat([values_of(b) for b in range(blocks)], 0)
    attended = dot_nn(w_ref[...], all_values).astype(BF16)
    for h in range(heads):
        att_ref[:, h * dim : (h + 1) * dim] = attended[h * tok : (h + 1) * tok]
    stores[0].start()
    send_own(0)

    all_keys = cat([keys_of(b) for b in range(blocks)], 0)
    gq = (dot_nn(ds_ref[...], all_keys) * scale).astype(BF16)
    for h in range(heads):
        gq_ref[:, h * dim : (h + 1) * dim] = gq[h * tok : (h + 1) * tok]
    stores[1].start()

    for copy in list(k_copies.values()) + list(v_copies.values()) + k_forwards + v_forwards:
        copy.wait_send()
    for copy in list(prev_copies.values()) + list(grad_copies.values()):
        copy.wait_send()
    for store in stores:
        store.wait()
    for copy in grad_copies.values():
        copy.wait_recv()


def store_kernel(
    group,
    att_hbm, gq_hbm, mine_hbm, recv_hbm, att_out, gq_out, gk_out, gv_out,
    att_ref, gq_ref, mine_ref, recv_ref, gk_ref, gv_ref, in_sem, out_sem,
):
    moves = ((mine_hbm, mine_ref), (recv_hbm, recv_ref), (att_hbm, att_ref), (gq_hbm, gq_ref))
    loads = [pltpu.make_async_copy(a, b, in_sem.at[n]) for n, (a, b) in enumerate(moves)]
    moves = ((att_ref, att_out), (gq_ref, gq_out), (gk_ref, gk_out), (gv_ref, gv_out))
    stores = [pltpu.make_async_copy(a, b, out_sem.at[n]) for n, (a, b) in enumerate(moves)]
    for load in loads:
        load.start()
    loads[0].wait()
    loads[1].wait()
    for part, out in ((0, gk_ref), (1, gv_ref)):
        total = mine_ref[part]
        for d in range(group - 1):
            total = total + recv_ref[part, d].astype(F32)
        out[...] = total.T.astype(BF16)
        stores[2 + part].start()
    for n in range(2):
        loads[2 + n].wait()
        stores[n].start()
    for store in stores:
        store.wait()


def solution(mesh):
    segments, group = mesh.shape["outer"], mesh.shape["inner"]

    def body(queries, key_vectors, value_vectors, grad_output, positions):
        tok, full = queries.shape
        dim = key_vectors.shape[1]
        heads = full // dim
        blocks, rows = 2 * group, heads * tok
        keys = blocks * tok
        wide, narrow = (tok, full), (tok, dim)
        scratch = [
            (wide, BF16),
            (wide, BF16),
            ((1, tok), jnp.int32),
            ((group, tok + 16, dim), BF16),
            ((group, tok, dim), BF16),
            ((group, tok, dim), BF16),
            ((group, tok, dim), BF16),
            ((rows, dim), BF16),
            ((rows, dim), BF16),
            ((dim, rows), BF16),
            ((dim, rows), BF16),
            ((rows, group * tok), F32),
            ((rows, group * tok), F32),
            ((rows, keys), BF16),
            ((rows, keys), BF16),
            ((2, group, dim, tok), BF16),
            ((2, group, dim, tok), BF16),
            ((2, group, dim, tok), BF16),
            ((2, group, dim, tok), F32),
            ((2, dim, tok), F32),
            (wide, BF16),
            (wide, BF16),
        ]
        made = [(wide, BF16), (wide, BF16), ((2, dim, tok), F32), ((2, group - 1, dim, tok), BF16)]
        results = [(wide, BF16), (wide, BF16), (narrow, BF16), (narrow, BF16)]
        hbm = pl.BlockSpec(memory_space=pl.ANY)
        sem = pltpu.SemaphoreType.DMA
        partial = pl.pallas_call(
            functools.partial(kernel, segments, group, heads, dim, tok),
            out_shape=[jax.ShapeDtypeStruct(s, t) for s, t in made],
            in_specs=[hbm] * 5,
            out_specs=[hbm] * 4,
            scratch_shapes=[pltpu.VMEM(s, t) for s, t in scratch]
            + [sem((5,)), sem((4,))]
            + [sem((group,))] * 8
            + [sem((2, group))] * 4,
            compiler_params=pltpu.CompilerParams(
                collective_id=0, has_side_effects=True, vmem_limit_bytes=vmem_bytes
            ),
            name="window_attention",
        )(queries, key_vectors, value_vectors, grad_output, positions.reshape(1, tok))
        return pl.pallas_call(
            functools.partial(store_kernel, group),
            out_shape=[jax.ShapeDtypeStruct(s, t) for s, t in results],
            in_specs=[hbm] * 4,
            out_specs=[hbm] * 4,
            scratch_shapes=[pltpu.VMEM(s, t) for s, t in made + results[2:]] + [sem((4,))] * 2,
            compiler_params=pltpu.CompilerParams(vmem_limit_bytes=vmem_bytes),
            name="store_results",
        )(*partial)

    rows = P(("outer", "inner"), None)
    return jax.shard_map(
        body,
        mesh=mesh,
        in_specs=(rows, rows, rows, rows, P(("outer", "inner"))),
        out_specs=(rows, rows, rows, rows),
        check_vma=False,
    )
```
